32 devices in a mesh: seq: 16 (over z, y, x), fsdp: 2 (over core).
Axes of the slice: x: 2, y: 2, z: 4, core: 2. Of those that a mesh axis runs over, the one named last changes fastest.
Arguments:
- probe_tensor: bfloat16 [2048, 2, 2048], P('seq', 'fsdp'), may hold values from -10 to 10
- matcher_tensor: bfloat16 [2048, 2, 2048], P('seq', 'fsdp'), may hold values from -10 to 10
- payload_tensor: bfloat16 [2048, 2, 2048], P('seq', 'fsdp'), may hold values from -6 to 6
- adjoint_attended: bfloat16 [2048, 2, 2048], P('seq', 'fsdp'), may hold values from -6 to 6
- logit_scale: float32 [16], replicated, may hold values from 0.5 to 2
- anchor_tiles: int32 [16, 2], replicated, may hold values from 0 to 31, as said below
- sampled_tiles: int32 [16, 32, 3], replicated, may hold values from 0 to 31, as said below
Outputs:
- query_gradients: bfloat16 [2048, 2, 2048], P('seq', 'fsdp')
- grad_key: bfloat16 [2048, 2, 2048], P('seq', 'fsdp')
- grad_value: bfloat16 [2048, 2, 2048], P('seq', 'fsdp')
- adjoint_scales: float32 [16], replicated
The draws below stay inside these ranges and needn't reach their ends.
Inputs may be any that keep to these rules, and one draw needn't show every extreme that they name: `anchor_tiles`: each head lists 2 different blocks. `sampled_tiles`: each row lists 3 different blocks, none within one block of the row's own block and none among the head's global blocks.
All inputs are finite; a program needn't handle non-finite values.
Results may differ from the reference program's by a relative error of at most 0.0083.
Values may be sent and summed in bfloat16 or wider, within the bound.
A program may use at most 64 MiB of HBM per device.

```python
import math
import jax
import jax.numpy as jnp
from jax import lax

CHANNEL_TOTAL = 16
HEAD_DIM = 128
TILE_SPAN = 64
GLOBALS = 2
RANDOM = 3
SEQ_TOK = 128
ATT_WIDTH = 2048
BATCH = 2
LENGTH = 2048
SHARES = 1
N_SEQ = 16


def drawn_pair(key):
    full_shape = (LENGTH, BATCH, CHANNEL_TOTAL * HEAD_DIM)
    drawn_query = jnp.clip(jax.random.normal(jax.random.fold_in(key, 101), full_shape, jnp.float32), -6.0, 6.0)
    drawn_key = jnp.clip(jax.random.normal(jax.random.fold_in(key, 102), full_shape, jnp.float32), -6.0, 6.0)
    return (drawn_query, drawn_key)


def draw_probe_tensor(key, part):
    return drawn_pair(key)[0].astype(jnp.bfloat16)


def draw_matcher_tensor(key, part):
    return drawn_pair(key)[1].astype(jnp.bfloat16)


def pick_globals(key):
    nblocks = LENGTH // TILE_SPAN
    col_ids = jnp.arange(nblocks, dtype=jnp.int32)
    int_score = jax.random.randint(jax.random.fold_in(key, 201), (CHANNEL_TOTAL, nblocks), 0, 1 << 20, dtype=jnp.int32) * nblocks + col_ids[None, :]
    return lax.top_k(int_score, GLOBALS)[1].astype(jnp.int32)


def draw_anchor_tiles(key, part):
    return pick_globals(key)


def draw_sampled_tiles(key, part):
    nblocks = LENGTH // TILE_SPAN
    glob_list = pick_globals(key)
    row_ids = jnp.arange(nblocks, dtype=jnp.int32)
    col_ids = jnp.arange(nblocks, dtype=jnp.int32)
    near_band = jnp.abs(row_ids[:, None] - col_ids[None, :]) <= 1
    is_global = jnp.any(glob_list[:, :, None] == col_ids[None, None, :], axis=1)
    banned = near_band[None, :, :] | is_global[:, None, :]
    int_score = jax.random.randint(jax.random.fold_in(key, 301), (CHANNEL_TOTAL, nblocks, nblocks), 0, 1 << 20, dtype=jnp.int32) * nblocks + col_ids[None, None, :]
    int_score = jnp.where(banned, -1, int_score)
    return lax.top_k(int_score, RANDOM)[1].astype(jnp.int32)


def steps_of(rng, extent, shards, low, high):
    def one(axis_at, parts):
        heights = jax.random.uniform(jax.random.fold_in(jax.random.fold_in(rng, 6), axis_at), (parts,), jnp.float32, low / len(shards), high / len(shards))
        return jnp.repeat(jnp.exp(heights), extent[axis_at] // parts).reshape((-1,) + (1,) * (len(extent) - axis_at - 1))

    factor_of = one(*shards[0])
    for cut in shards[1:]:
        factor_of = factor_of * one(*cut)
    return factor_of


def gaussian(stream_key, dims, deviation, limit, shards=(), kind=jnp.bfloat16):
    loudness = steps_of(stream_key, dims, shards, -0.22, 0.18) if shards else 1.0
    entries = jax.random.normal(stream_key, dims, jnp.float32) * deviation * loudness
    return jnp.minimum(jnp.maximum(entries, -limit), limit).astype(kind)


def setup_inputs(seed: int = 0) -> dict:
    key_of = jax.random.split(jax.random.key(seed), 8)
    return {
        "probe_tensor": draw_probe_tensor(jax.random.fold_in(key_of[7], 71), 0),
        "matcher_tensor": draw_matcher_tensor(jax.random.fold_in(key_of[7], 71), 0),
        "payload_tensor": gaussian(key_of[2], (LENGTH, BATCH, ATT_WIDTH), 1.0, 6.0, ((0, 16), (1, 2))),
        "adjoint_attended": gaussian(key_of[3], (LENGTH, BATCH, ATT_WIDTH), 1.0, 6.0, ((0, 16), (1, 2))),
        "logit_scale": jnp.clip(jnp.exp(jax.random.uniform(key_of[4], (CHANNEL_TOTAL,), jnp.float32, math.log(0.5), math.log(2.0))), 0.5, 2.0),
        "anchor_tiles": draw_anchor_tiles(jax.random.fold_in(key_of[7], 71), 0),
        "sampled_tiles": draw_sampled_tiles(jax.random.fold_in(key_of[7], 71), 0),
    }


masked_minimum = -1e+30

def group_of(count):
    for size in (8, 4, 2):
        if count % size == 0:
            return size
    return 1

def block_lists(anchor_tiles, sampled_tiles, nblocks):
    channel_roster = anchor_tiles.shape[0]
    block_ids = jnp.arange(nblocks, dtype=jnp.int32)
    offsets = jnp.array([-1, 0, 1], dtype=jnp.int32)
    window = jnp.broadcast_to((block_ids[:, None] + offsets[None, :])[None], (channel_roster, nblocks, 3))
    window_ok = (window >= 0) & (window < nblocks)
    glob_slots = jnp.broadcast_to(anchor_tiles[:, None, :], (channel_roster, nblocks, anchor_tiles.shape[1])).astype(jnp.int32)
    glob_ok = jnp.abs(glob_slots - block_ids[None, :, None]) > 1
    rand_ok = jnp.ones(sampled_tiles.shape, dtype=bool)
    position_pointer = jnp.concatenate([window, glob_slots, sampled_tiles.astype(jnp.int32)], axis=2)
    position_pointer = jnp.clip(position_pointer, 0, nblocks - 1).astype(jnp.int32)
    position_usable = jnp.concatenate([window_ok, glob_ok, rand_ok], axis=2)
    return (position_pointer, position_usable)

def share_units(device_portion, tok_local, seq_parts, copies, tile_index, tile_span):
    piece = tok_local // copies
    per_piece = piece // tile_index
    units = jnp.arange(seq_parts * per_piece, dtype=jnp.int32)
    position = units // per_piece * tok_local + device_portion * piece + units % per_piece * tile_index
    return (position // tile_span).astype(jnp.int32)

def attend_sample(probe_vector, matcher_tiles, payload_tiles, adjoint_signal, channel_scale, position_pointer, position_usable, tile_index, tile_span):
    q_len, channel_width = probe_vector.shape
    k_len = matcher_tiles.shape[0]
    q_units = q_len // tile_index
    k_blocks = k_len // tile_span
    group_size = group_of(q_units)
    group_count = q_units // group_size
    reciprocal_sqrt_width = 1.0 / math.sqrt(channel_width)
    key_blocks = matcher_tiles.reshape(k_blocks, tile_span, channel_width).astype(jnp.float32)
    value_blocks = payload_tiles.reshape(k_blocks, tile_span, channel_width).astype(jnp.float32)
    q_groups = probe_vector.reshape(group_count, group_size, tile_index, channel_width).astype(jnp.float32)
    g_groups = adjoint_signal.reshape(group_count, group_size, tile_index, channel_width).astype(jnp.float32)
    i_groups = position_pointer.reshape(group_count, group_size, -1)
    v_groups = position_usable.reshape(group_count, group_size, -1)

    def step(carried, inputs):
        key_acc, value_acc, temp_acc = carried
        q_blk, g_blk, idx_blk, ok_blk = inputs
        k_sel = key_blocks[idx_blk]
        v_sel = value_blocks[idx_blk]
        logit_matrix = jnp.einsum('gbd,gsjd->gbsj', q_blk, k_sel) * reciprocal_sqrt_width
        position_filter = ok_blk[:, None, :, None]
        rescaled_logits = jnp.where(position_filter, channel_scale * logit_matrix, masked_minimum)
        row_max = lax.optimization_barrier(jnp.max(rescaled_logits, axis=(2, 3), keepdims=True))
        expo_terms = jnp.where(position_filter, jnp.exp(rescaled_logits - row_max), 0.0)
        row_total = lax.optimization_barrier(jnp.sum(expo_terms, axis=(2, 3), keepdims=True))
        attn_prob = expo_terms / row_total
        prob_low = attn_prob.astype(jnp.bfloat16).astype(jnp.float32)
        d_prob = jnp.einsum('gbd,gsjd->gbsj', g_blk, v_sel)
        row_delta = lax.optimization_barrier(jnp.sum(attn_prob * d_prob, axis=(2, 3), keepdims=True))
        adjoint_weights = attn_prob * (d_prob - row_delta)
        temp_acc = temp_acc + jnp.sum(adjoint_weights * logit_matrix)
        adjoint_logits = (adjoint_weights * (channel_scale * reciprocal_sqrt_width)).astype(jnp.bfloat16).astype(jnp.float32)
        adjoint_probe = jnp.einsum('gbsj,gsjd->gbd', adjoint_logits, k_sel)
        d_keys = jnp.einsum('gbsj,gbd->gsjd', adjoint_logits, q_blk)
        d_values = jnp.einsum('gbsj,gbd->gsjd', prob_low, g_blk)
        key_acc = key_acc.at[idx_blk].add(d_keys)
        value_acc = value_acc.at[idx_blk].add(d_values)
        return ((key_acc, value_acc, temp_acc), adjoint_probe.astype(jnp.bfloat16))
    start = (jnp.zeros((k_blocks, tile_span, channel_width), jnp.float32), jnp.zeros((k_blocks, tile_span, channel_width), jnp.float32), jnp.zeros((), jnp.float32))
    (key_acc, value_acc, temp_acc), adjoint_probe = lax.scan(step, start, (q_groups, g_groups, i_groups, v_groups))
    return (adjoint_probe.reshape(q_len, channel_width), key_acc.reshape(k_len, channel_width).astype(jnp.bfloat16), value_acc.reshape(k_len, channel_width).astype(jnp.bfloat16), temp_acc)

def reference(probe_tensor, matcher_tensor, payload_tensor, adjoint_attended, logit_scale, anchor_tiles, sampled_tiles):
    length, batch, width = probe_tensor.shape
    channel_roster = logit_scale.shape[0]
    channel_width = width // channel_roster
    nblocks = length // TILE_SPAN
    position_pointer, position_usable = block_lists(anchor_tiles, sampled_tiles, nblocks)
    piece = SEQ_TOK // SHARES
    tile_index = min(TILE_SPAN, piece)

    def to_samples(array):
        return array.reshape(length, batch * channel_roster, channel_width).transpose(1, 0, 2)
    channel_finder = jnp.arange(batch * channel_roster, dtype=jnp.int32) % channel_roster

    def sample_mapped(sample_operands):
        probe_vector, matcher_tiles, payload_tiles, adjoint_signal, channel_ordinal = sample_operands
        channel_scale = logit_scale[channel_ordinal]
        sample_indices = position_pointer[channel_ordinal]
        sample_valid_mask = position_usable[channel_ordinal]
        probe_pieces = probe_vector.reshape(N_SEQ, SHARES, piece, channel_width)
        adjoint_pieces = adjoint_signal.reshape(N_SEQ, SHARES, piece, channel_width)
        query_parts = []
        key_total = jnp.zeros((length, channel_width), jnp.float32)
        value_total = jnp.zeros((length, channel_width), jnp.float32)
        scale_accumulator = jnp.zeros((), jnp.float32)
        for device_portion in range(SHARES):
            tiles_per_device = share_units(device_portion, SEQ_TOK, N_SEQ, SHARES, tile_index, TILE_SPAN)
            adjoint_probe, adjoint_matcher, adjoint_payload, adjoint_scale = attend_sample(probe_pieces[:, device_portion].reshape(-1, channel_width), matcher_tiles, payload_tiles, adjoint_pieces[:, device_portion].reshape(-1, channel_width), channel_scale, sample_indices[tiles_per_device], sample_valid_mask[tiles_per_device], tile_index, TILE_SPAN)
            query_parts.append(adjoint_probe.reshape(N_SEQ, 1, piece, channel_width))
            key_total = key_total + adjoint_matcher.astype(jnp.float32)
            value_total = value_total + adjoint_payload.astype(jnp.float32)
            scale_accumulator = scale_accumulator + adjoint_scale
        return (jnp.concatenate(query_parts, axis=1).reshape(length, channel_width), key_total.astype(jnp.bfloat16), value_total.astype(jnp.bfloat16), scale_accumulator)
    adjoint_probe, adjoint_matcher, adjoint_payload, adjoint_scale = lax.map(sample_mapped, (to_samples(probe_tensor), to_samples(matcher_tensor), to_samples(payload_tensor), to_samples(adjoint_attended), channel_finder))

    def to_flat_sequence(array):
        return array.transpose(1, 0, 2).reshape(length, batch, width)
    adjoint_scales = jax.ops.segment_sum(adjoint_scale, channel_finder, num_segments=channel_roster)
    return (to_flat_sequence(adjoint_probe), to_flat_sequence(adjoint_matcher), to_flat_sequence(adjoint_payload), adjoint_scales)
```

```python
import functools
import math

import jax
import jax.numpy as jnp
from jax import lax
from jax.experimental import pallas as pl
from jax.experimental.pallas import tpu as pltpu
from jax.sharding import PartitionSpec as P

TILE_SPAN = 64
MASKED = -1e30
MESH = pl.DeviceIdType.MESH
F32 = jnp.float32
BF16 = jnp.bfloat16


def attention_kernel(
    dims,
    q_in,
    k_in,
    v_in,
    g_in,
    scale_in,
    table,
    q_out,
    k_out,
    v_out,
    scale_out,
    qbuf,
    kbuf,
    vbuf,
    gbuf,
    s_ref,
    p_ref,
    dk_acc,
    dv_acc,
    dk_anchor,
    dv_anchor,
    dk_chain,
    dv_chain,
    dq_send,
    dk_send,
    dv_send,
    temp_acc,
    pair_terms,
    item_terms,
    in_send,
    in_recv,
    out_send,
    out_recv,
    term_send,
    term_recv,
):
    n, nf, copies, tok, piece, tile, width, heads, n_anchor, n_random = dims
    span = TILE_SPAN
    nblocks = n * tok // span
    units = piece // tile
    entries = n * units * n_random
    window = 3 * span
    reciprocal = 1.0 / math.sqrt(width)
    me = lax.axis_index("seq")
    mine = lax.axis_index("fsdp")
    item = me // copies
    replica = me % copies
    cols = lambda d: pl.ds(pl.multiple_of(d // copies * width, width), width)

    barrier = pltpu.get_barrier_semaphore()

    def greet(o, _):
        pl.semaphore_signal(
            barrier, inc=1, device_id={"seq": (me + o) % n}, device_id_type=MESH
        )
        return _

    lax.fori_loop(1, n, greet, 0)
    for o in range(1, nf):
        pl.semaphore_signal(
            barrier, inc=1, device_id={"fsdp": (mine + o) % nf}, device_id_type=MESH
        )
    pl.semaphore_wait(barrier, n - 1 + nf - 1)

    arrivals = (
        (k_in, kbuf, tok // span, 1),
        (q_in, qbuf, piece, 0),
        (g_in, gbuf, piece, 0),
        (v_in, vbuf, tok // span, 1),
    )
    for a, (source, target, rows, shift) in enumerate(arrivals):

        def block(d):
            if shift:
                return source.at[:, :, cols(d)]
            return source.at[pl.ds(pl.multiple_of(d % copies * rows, rows), rows), cols(d)]

        if shift:
            landing = target.at[pl.ds(shift + me * rows, rows)]
        else:
            landing = target.at[pl.ds(pl.multiple_of(me * rows, rows), rows)]

        def send(o, _):
            d = (me + o) % n
            pltpu.make_async_remote_copy(
                src_ref=block(d),
                dst_ref=landing,
                send_sem=in_send.at[a],
                recv_sem=in_recv.at[a],
                device_id={"seq": d},
                device_id_type=MESH,
            ).start()
            return _

        pltpu.make_async_copy(block(me), landing, in_recv.at[a]).start()
        lax.fori_loop(1, n, send, 0)

    def arrive(a):
        _, target, rows, shift = arrivals[a]
        ref = target.at[pl.ds(shift, n * rows)]
        pltpu.make_async_copy(ref, ref, in_recv.at[a]).wait()

    zero_block = jnp.zeros((span, width), BF16)
    for buf in (kbuf, vbuf):
        buf[0] = zero_block
        buf[nblocks + 1] = zero_block

    def clear(c, _):
        dk_acc[c] = jnp.zeros((span, width), F32)
        dv_acc[c] = jnp.zeros((span, width), F32)
        return _

    lax.fori_loop(0, nblocks + 2, clear, 0)
    dk_anchor[...] = jnp.zeros_like(dk_anchor)
    dv_anchor[...] = jnp.zeros_like(dv_anchor)
    dk_chain[0] = jnp.zeros((span, width), F32)
    dv_chain[0] = jnp.zeros((span, width), F32)
    temp_acc[...] = jnp.zeros_like(temp_acc)

    scale = scale_in[item % heads]
    alpha = scale * reciprocal
    anchors = [table[2 * entries + nblocks + x] for x in range(n_anchor)]
    slots = 3 + n_anchor + n_random
    slot_of = lax.broadcasted_iota(jnp.int32, (1, slots * span), 1) // span

    def unit_at(k, j):
        p = (me + 1 + k) % n
        row = pl.multiple_of(p * piece + j * tile, tile)
        blk = (p * tok + replica * piece + j * tile) // span
        return pl.ds(row, tile), blk, k * units + j

    def select(buf, blk, t):
        parts = [buf[pl.ds(blk, 3)].reshape(window, width)]
        for a in anchors:
            parts.append(buf[a + 1])
        for x in range(n_random):
            parts.append(buf[table[t * n_random + x] + 1])
        return jnp.concatenate(parts, axis=0)

    def bias_of(blk):
        off = lambda dead: jnp.where(dead, MASKED, 0.0).astype(F32)
        bias = jnp.where(slot_of == 0, off(blk == 0), 0.0)
        bias = jnp.where(slot_of == 2, off(blk == nblocks - 1), bias)
        for x, a in enumerate(anchors):
            bias = jnp.where(slot_of == 3 + x, off(jnp.abs(a - blk) <= 1), bias)
        return bias

    def scatter(got, places, acc, anchor, chain):
        base = window + n_anchor * span
        for (blk, t), d in zip(places, got):
            acc[pl.ds(blk, 3)] += d[:window].reshape(3, span, width)
            anchor[...] += d[window:base].reshape(n_anchor, span, width)
            for x in range(n_random):
                e = t * n_random + x
                before = table[entries + e]
                chain[e + 1] = chain[before] + d[base + x * span : base + (x + 1) * span]

    rows_by_cols = (((1,), (1,)), ((), ()))
    over_rows = (((0,), (0,)), ((), ()))

    arrive(0)
    arrive(1)

    def scores(k, _):
        for j in range(units):
            at, blk, t = unit_at(k, j)
            s = lax.dot_general(
                qbuf[at, :], select(kbuf, blk, t), rows_by_cols, preferred_element_type=F32
            )
            logits = s * alpha + bias_of(blk)
            e = jnp.exp(logits - jnp.max(logits, axis=1, keepdims=True))
            s_ref[at, :] = s
            p_ref[at, :] = e * (1.0 / jnp.sum(e, axis=1, keepdims=True))
        return _

    lax.fori_loop(0, n, scores, 0)

    arrive(2)

    def value_terms(k, _):
        got, places = [], []
        for j in range(units):
            at, blk, t = unit_at(k, j)
            low = p_ref[at, :].astype(BF16)
            got.append(
                lax.dot_general(low, gbuf[at, :], over_rows, preferred_element_type=F32)
            )
            places.append((blk, t))
        scatter(got, places, dv_acc, dv_anchor, dv_chain)
        return _

    lax.fori_loop(0, n, value_terms, 0)

    def send_back(source, rows, target, target_rows, x, k):
        d = (me + 1 + k) % n
        block = source.at[pl.ds(pl.multiple_of(d * rows, rows), rows)]

        @pl.when(k < n - 1)
        def _():
            pltpu.make_async_remote_copy(
                src_ref=block,
                dst_ref=target.at[target_rows, landing_cols[x]],
                send_sem=out_send.at[x],
                recv_sem=out_recv.at[x],
                device_id={"seq": d},
                device_id_type=MESH,
            ).start()

        @pl.when(k == n - 1)
        def _():
            pltpu.make_async_copy(
                source.at[pl.ds(pl.multiple_of(me * rows, rows), rows)],
                target.at[target_rows, landing_cols[x]],
                out_recv.at[x],
            ).start()

    own_part = pl.ds(pl.multiple_of(me * width, width), width)
    landing_cols = (cols(me), own_part, own_part)

    def finish(acc, anchor, chain, source, target, x):
        def step(k, _):
            d = (me + 1 + k) % n
            for b in range(tok // span):
                c = d * (tok // span) + b
                last = table[2 * entries + c]
                total = acc[c + 1] + chain[last]
                for y, a in enumerate(anchors):
                    total += jnp.where(a == c, anchor[y], 0.0)
                source[pl.ds(pl.multiple_of(c * span, span), span), :] = total.astype(BF16)
            send_back(source, tok, target, slice(None), x, k)
            return _

        lax.fori_loop(0, n, step, 0)

    finish(dv_acc, dv_anchor, dv_chain, dv_send, v_out, 2)

    arrive(3)

    def score_terms(k, _):
        got, places = [], []
        for j in range(units):
            at, blk, t = unit_at(k, j)
            dprob = lax.dot_general(
                gbuf[at, :], select(vbuf, blk, t), rows_by_cols, preferred_element_type=F32
            )
            prob = p_ref[at, :]
            delta = jnp.sum(prob * dprob, axis=1, keepdims=True)
            dscore = prob * (dprob - delta)
            both = dscore * s_ref[at, :]
            lanes = both[:, :width]
            for y in range(1, slots * span // width):
                lanes += both[:, y * width : (y + 1) * width]
            part = lanes[0:8]
            for y in range(1, tile // 8):
                part += lanes[y * 8 : (y + 1) * 8]
            temp_acc[...] += part
            draw = (dscore * alpha).astype(BF16)
            dq = jnp.dot(draw, select(kbuf, blk, t), preferred_element_type=F32)
            dq_send[at, :] = dq.astype(BF16)
            got.append(
                lax.dot_general(draw, qbuf[at, :], over_rows, preferred_element_type=F32)
            )
            places.append((blk, t))
        mine_rows = pl.ds(pl.multiple_of(replica * piece, piece), piece)
        send_back(dq_send, piece, q_out, mine_rows, 0, k)
        scatter(got, places, dk_acc, dk_anchor, dk_chain)
        return _

    lax.fori_loop(0, n, score_terms, 0)
    finish(dk_acc, dk_anchor, dk_chain, dk_send, k_out, 1)

    total = jnp.sum(temp_acc[...], axis=1, keepdims=True)
    total = jnp.sum(total, axis=0, keepdims=True) * reciprocal
    pair_terms[mine] = jnp.broadcast_to(total, (8, 128))
    for o in range(1, nf):
        pltpu.make_async_remote_copy(
            src_ref=pair_terms.at[mine],
            dst_ref=pair_terms.at[mine],
            send_sem=term_send.at[0],
            recv_sem=term_recv.at[0],
            device_id={"fsdp": (mine + o) % nf},
            device_id_type=MESH,
        ).start()
    rest = pair_terms.at[pl.ds(0, nf - 1)]
    pltpu.make_async_copy(rest, rest, term_recv.at[0]).wait()
    pltpu.make_async_copy(rest, rest, term_send.at[0]).wait()
    total = pair_terms[0]
    for o in range(1, nf):
        total += pair_terms[o]
    item_terms[me] = total

    def tell(o, _):
        pltpu.make_async_remote_copy(
            src_ref=item_terms.at[me],
            dst_ref=item_terms.at[me],
            send_sem=term_send.at[1],
            recv_sem=term_recv.at[1],
            device_id={"seq": (me + o) % n},
            device_id_type=MESH,
        ).start()
        return _

    lax.fori_loop(1, n, tell, 0)
    rest = item_terms.at[pl.ds(0, n - 1)]
    pltpu.make_async_copy(rest, rest, term_recv.at[1]).wait()
    pltpu.make_async_copy(rest, rest, term_send.at[1]).wait()
    lane = lax.broadcasted_iota(jnp.int32, (8, 128), 1)
    result = jnp.zeros((8, 128), F32)
    for d in range(n):
        result += jnp.where(lane == d // copies % heads, item_terms[d], 0.0)
    scale_out[...] = result

    for a, (_, target, rows, _) in enumerate(arrivals):
        ref = target.at[pl.ds(0, (n - 1) * rows)]
        pltpu.make_async_copy(ref, ref, in_send.at[a]).wait()
    for x, (source, rows, target) in enumerate(
        ((dq_send, piece, q_out), (dk_send, tok, k_out), (dv_send, tok, v_out))
    ):
        ref = source.at[pl.ds(0, (n - 1) * rows)]
        pltpu.make_async_copy(ref, ref, out_send.at[x]).wait()
        pltpu.make_async_copy(target, target, out_recv.at[x]).wait()


def slot_table(anchor_tiles, sampled_tiles, head, blocks, nblocks):
    tiles = jnp.take(lax.dynamic_index_in_dim(sampled_tiles, head, 0, False), blocks, axis=0)
    tiles = tiles.reshape(-1).astype(jnp.int32)
    place = jnp.arange(tiles.shape[0], dtype=jnp.int32)
    earlier = (tiles[:, None] == tiles[None, :]) & (place[None, :] < place[:, None])
    before = jnp.max(jnp.where(earlier, place[None, :] + 1, 0), axis=1)
    ids = jnp.arange(nblocks, dtype=jnp.int32)
    last = jnp.max(jnp.where(tiles[None, :] == ids[:, None], place[None, :] + 1, 0), axis=1)
    anchors = lax.dynamic_index_in_dim(anchor_tiles, head, 0, False).astype(jnp.int32)
    return jnp.concatenate([tiles, before, last, anchors])


def on_device(n, nf, probe, matcher, payload, adjoint, logit_scale, anchor_tiles, sampled_tiles):
    tok, seq_count, total_width = probe.shape
    heads = logit_scale.shape[0]
    width = total_width // heads
    copies = n // (seq_count * heads)
    assert seq_count == 1 and copies * heads == n
    piece = tok // copies
    tile = min(TILE_SPAN, piece)
    units = piece // tile
    n_anchor, n_random = anchor_tiles.shape[1], sampled_tiles.shape[2]
    nblocks = n * tok // TILE_SPAN
    me = lax.axis_index("seq")
    order = jnp.arange(n * units, dtype=jnp.int32)
    peer = (me + 1 + order // units) % n
    blocks = (peer * tok + me % copies * piece + order % units * tile) // TILE_SPAN
    table = slot_table(anchor_tiles, sampled_tiles, me // copies % heads, blocks, nblocks)

    dims = (n, nf, copies, tok, piece, tile, width, heads, n_anchor, n_random)
    keys = n * tok
    queries = n * piece
    slots = (3 + n_anchor + n_random) * TILE_SPAN
    chain = (n * units * n_random + 1, TILE_SPAN, width)
    padded = (nblocks + 2, TILE_SPAN, width)
    anywhere = pl.BlockSpec(memory_space=pl.ANY)
    scalars = pl.BlockSpec(memory_space=pltpu.SMEM)
    flat = lambda array: array.reshape(tok, total_width)
    tiled = lambda array: array.reshape(tok // TILE_SPAN, TILE_SPAN, total_width)
    parts = jax.ShapeDtypeStruct((tok, n * width), BF16)
    q_out, k_out, v_out, scales = pl.pallas_call(
        functools.partial(attention_kernel, dims),
        out_shape=(
            jax.ShapeDtypeStruct((tok, total_width), BF16),
            parts,
            parts,
            jax.ShapeDtypeStruct((8, 128), F32),
        ),
        in_specs=[anywhere] * 4 + [scalars] * 2,
        out_specs=(anywhere, anywhere, anywhere, pl.BlockSpec(memory_space=pltpu.VMEM)),
        scratch_shapes=[
            pltpu.VMEM((queries, width), BF16),
            pltpu.VMEM(padded, BF16),
            pltpu.VMEM(padded, BF16),
            pltpu.VMEM((queries, width), BF16),
            pltpu.VMEM((queries, slots), F32),
            pltpu.VMEM((queries, slots), F32),
            pltpu.VMEM(padded, F32),
            pltpu.VMEM(padded, F32),
            pltpu.VMEM((n_anchor, TILE_SPAN, width), F32),
            pltpu.VMEM((n_anchor, TILE_SPAN, width), F32),
            pltpu.VMEM(chain, F32),
            pltpu.VMEM(chain, F32),
            pltpu.VMEM((queries, width), BF16),
            pltpu.VMEM((keys, width), BF16),
            pltpu.VMEM((keys, width), BF16),
            pltpu.VMEM((8, 128), F32),
            pltpu.VMEM((nf, 8, 128), F32),
            pltpu.VMEM((n, 8, 128), F32),
            pltpu.SemaphoreType.DMA((4,)),
            pltpu.SemaphoreType.DMA((4,)),
            pltpu.SemaphoreType.DMA((3,)),
            pltpu.SemaphoreType.DMA((3,)),
            pltpu.SemaphoreType.DMA((2,)),
            pltpu.SemaphoreType.DMA((2,)),
        ],
        compiler_params=pltpu.CompilerParams(
            collective_id=0, has_side_effects=True, vmem_limit_bytes=56 * 1024 * 1024
        ),
        cost_estimate=pl.CostEstimate(
            flops=10 * queries * slots * width,
            bytes_accessed=14 * tok * total_width,
            transcendentals=queries * slots,
        ),
    )(flat(probe), tiled(matcher), tiled(payload), flat(adjoint), logit_scale, table)

    def combine(received):
        if copies > 1:
            pieces = received.astype(F32).reshape(tok, heads, copies, width)
            received = jnp.sum(pieces, axis=2).astype(BF16)
        return received.reshape(tok, seq_count, total_width)

    return q_out.reshape(probe.shape), combine(k_out), combine(v_out), scales[0, :heads]


def solution(mesh):
    placed = P("seq", "fsdp", None)
    return jax.shard_map(
        functools.partial(on_device, mesh.shape["seq"], mesh.shape["fsdp"]),
        mesh=mesh,
        in_specs=(placed, placed, placed, placed, P(), P(), P()),
        out_specs=(placed, placed, placed, P()),
        check_vma=False,
    )
```

```python
import functools
import math

import jax
import jax.numpy as jnp
from jax import lax
from jax.experimental import pallas as pl
from jax.experimental.pallas import tpu as pltpu
from jax.sharding import PartitionSpec as P

TILE_SPAN = 64
MASKED = -1e30
MESH = pl.DeviceIdType.MESH
F32 = jnp.float32
BF16 = jnp.bfloat16


def attention_kernel(
    dims,
    q_in,
    k_in,
    v_in,
    g_in,
    scale_in,
    table,
    q_out,
    k_out,
    v_out,
    scale_out,
    qbuf,
    kbuf,
    vbuf,
    gbuf,
    s_ref,
    p_ref,
    dk_acc,
    dv_acc,
    dk_anchor,
    dv_anchor,
    dk_chain,
    dv_chain,
    dq_send,
    dk_send,
    dv_send,
    temp_acc,
    pair_terms,
    item_terms,
    in_send,
    in_recv,
    out_send,
    out_recv,
    term_send,
    term_recv,
):
    n, nf, copies, tok, piece, tile, width, heads, n_anchor, n_random = dims
    span = TILE_SPAN
    nblocks = n * tok // span
    units = piece // tile
    entries = n * units * n_random
    window = 3 * span
    reciprocal = 1.0 / math.sqrt(width)
    me = lax.axis_index("seq")
    mine = lax.axis_index("fsdp")
    item = me // copies
    replica = me % copies
    cols = lambda d: pl.ds(pl.multiple_of(d // copies * width, width), width)

    barrier = pltpu.get_barrier_semaphore()

    def greet(o, _):
        pl.semaphore_signal(
            barrier, inc=1, device_id={"seq": (me + o) % n}, device_id_type=MESH
        )
        return _

    lax.fori_loop(1, n, greet, 0)
    for o in range(1, nf):
        pl.semaphore_signal(
            barrier, inc=1, device_id={"fsdp": (mine + o) % nf}, device_id_type=MESH
        )
    pl.semaphore_wait(barrier, n - 1 + nf - 1)

    arrivals = (
        (k_in, kbuf, tok // span, 1),
        (q_in, qbuf, piece, 0),
        (g_in, gbuf, piece, 0),
        (v_in, vbuf, tok // span, 1),
    )

    def prepare():
        zero_block = jnp.zeros((span, width), BF16)
        for buf in (kbuf, vbuf):
            buf[0] = zero_block
            buf[nblocks + 1] = zero_block

        def clear(c, _):
            dk_acc[c] = jnp.zeros((span, width), F32)
            dv_acc[c] = jnp.zeros((span, width), F32)
            return _

        lax.fori_loop(0, nblocks + 2, clear, 0)
        dk_anchor[...] = jnp.zeros_like(dk_anchor)
        dv_anchor[...] = jnp.zeros_like(dv_anchor)
        dk_chain[0] = jnp.zeros((span, width), F32)
        dv_chain[0] = jnp.zeros((span, width), F32)
        temp_acc[...] = jnp.zeros_like(temp_acc)

    def sent(a):
        _, target, rows, _ = arrivals[a]
        ref = target.at[pl.ds(0, (n - 1) * rows)]
        pltpu.make_async_copy(ref, ref, in_send.at[a]).wait()

    for a, (source, target, rows, shift) in enumerate(arrivals):
        if a == 2:
            prepare()
        if a >= 2:
            sent(a - 2)

        def block(d):
            if shift:
                return source.at[:, :, cols(d)]
            return source.at[pl.ds(pl.multiple_of(d % copies * rows, rows), rows), cols(d)]

        if shift:
            landing = target.at[pl.ds(shift + me * rows, rows)]
        else:
            landing = target.at[pl.ds(pl.multiple_of(me * rows, rows), rows)]

        def send(o, _):
            d = (me + o) % n
            pltpu.make_async_remote_copy(
                src_ref=block(d),
                dst_ref=landing,
                send_sem=in_send.at[a],
                recv_sem=in_recv.at[a],
                device_id={"seq": d},
                device_id_type=MESH,
            ).start()
            return _

        pltpu.make_async_copy(block(me), landing, in_recv.at[a]).start()
        lax.fori_loop(1, n, send, 0)

    def arrive(a):
        _, target, rows, shift = arrivals[a]
        ref = target.at[pl.ds(shift, n * rows)]
        pltpu.make_async_copy(ref, ref, in_recv.at[a]).wait()

    scale = scale_in[item % heads]
    alpha = scale * reciprocal
    anchors = [table[2 * entries + nblocks + x] for x in range(n_anchor)]
    slots = 3 + n_anchor + n_random
    slot_of = lax.broadcasted_iota(jnp.int32, (1, slots * span), 1) // span

    def unit_at(k, j):
        p = (me + 1 + k) % n
        row = pl.multiple_of(p * piece + j * tile, tile)
        blk = (p * tok + replica * piece + j * tile) // span
        return pl.ds(row, tile), blk, k * units + j

    def select(buf, blk, t):
        parts = [buf[pl.ds(blk, 3)].reshape(window, width)]
        for a in anchors:
            parts.append(buf[a + 1])
        for x in range(n_random):
            parts.append(buf[table[t * n_random + x] + 1])
        return jnp.concatenate(parts, axis=0)

    def bias_of(blk):
        off = lambda dead: jnp.where(dead, MASKED, 0.0).astype(F32)
        bias = jnp.where(slot_of == 0, off(blk == 0), 0.0)
        bias = jnp.where(slot_of == 2, off(blk == nblocks - 1), bias)
        for x, a in enumerate(anchors):
            bias = jnp.where(slot_of == 3 + x, off(jnp.abs(a - blk) <= 1), bias)
        return bias

    def scatter(got, places, acc, anchor, chain):
        base = window + n_anchor * span
        for (blk, t), d in zip(places, got):
            acc[pl.ds(blk, 3)] += d[:window].reshape(3, span, width)
            anchor[...] += d[window:base].reshape(n_anchor, span, width)
            for x in range(n_random):
                e = t * n_random + x
                before = table[entries + e]
                chain[e + 1] = chain[before] + d[base + x * span : base + (x + 1) * span]

    rows_by_cols = (((1,), (1,)), ((), ()))
    over_rows = (((0,), (0,)), ((), ()))

    arrive(0)
    arrive(1)

    group = 2 if units <= 2 else 1
    steps = n // group
    members = lambda i: [(i * group + y, j) for y in range(group) for j in range(units)]

    def scores(i, _):
        for k, j in members(i):
            at, blk, t = unit_at(k, j)
            s = lax.dot_general(
                qbuf[at, :], select(kbuf, blk, t), rows_by_cols, preferred_element_type=F32
            )
            logits = s * alpha + bias_of(blk)
            e = jnp.exp(logits - jnp.max(logits, axis=1, keepdims=True))
            s_ref[at, :] = s
            p_ref[at, :] = e * (1.0 / jnp.sum(e, axis=1, keepdims=True))
        return _

    lax.fori_loop(0, steps, scores, 0)

    arrive(2)

    def value_terms(i, _):
        got, places = [], []
        for k, j in members(i):
            at, blk, t = unit_at(k, j)
            low = p_ref[at, :].astype(BF16)
            got.append(
                lax.dot_general(low, gbuf[at, :], over_rows, preferred_element_type=F32)
            )
            places.append((blk, t))
        scatter(got, places, dv_acc, dv_anchor, dv_chain)
        return _

    lax.fori_loop(0, steps, value_terms, 0)

    def send_back(source, rows, target, target_rows, x, k):
        d = (me + 1 + k) % n
        block = source.at[pl.ds(pl.multiple_of(d * rows, rows), rows)]

        @pl.when(k < n - 1)
        def _():
            pltpu.make_async_remote_copy(
                src_ref=block,
                dst_ref=target.at[target_rows, landing_cols[x]],
                send_sem=out_send.at[x],
                recv_sem=out_recv.at[x],
                device_id={"seq": d},
                device_id_type=MESH,
            ).start()

        @pl.when(k == n - 1)
        def _():
            pltpu.make_async_copy(
                source.at[pl.ds(pl.multiple_of(me * rows, rows), rows)],
                target.at[target_rows, landing_cols[x]],
                out_recv.at[x],
            ).start()

    own_part = pl.ds(pl.multiple_of(me * width, width), width)
    landing_cols = (cols(me), own_part, own_part)

    def finish(acc, anchor, chain, source, target, x):
        def step(k, _):
            d = (me + 1 + k) % n
            for b in range(tok // span):
                c = d * (tok // span) + b
                last = table[2 * entries + c]
                total = acc[c + 1] + chain[last]
                for y, a in enumerate(anchors):
                    total += jnp.where(a == c, anchor[y], 0.0)
                source[pl.ds(pl.multiple_of(c * span, span), span), :] = total.astype(BF16)
            send_back(source, tok, target, slice(None), x, k)
            return _

        lax.fori_loop(0, n, step, 0)

    finish(dv_acc, dv_anchor, dv_chain, dv_send, v_out, 2)

    arrive(3)

    def score_terms(i, _):
        got, places = [], []
        for k, j in members(i):
            at, blk, t = unit_at(k, j)
            dprob = lax.dot_general(
                gbuf[at, :], select(vbuf, blk, t), rows_by_cols, preferred_element_type=F32
            )
            prob = p_ref[at, :]
            delta = jnp.sum(prob * dprob, axis=1, keepdims=True)
            dscore = prob * (dprob - delta)
            both = dscore * s_ref[at, :]
            lanes = both[:, :width]
            for y in range(1, slots * span // width):
                lanes += both[:, y * width : (y + 1) * width]
            part = lanes[0:8]
            for y in range(1, tile // 8):
                part += lanes[y * 8 : (y + 1) * 8]
            temp_acc[...] += part
            draw = (dscore * alpha).astype(BF16)
            dq = jnp.dot(draw, select(kbuf, blk, t), preferred_element_type=F32)
            dq_send[at, :] = dq.astype(BF16)
            got.append(
                lax.dot_general(draw, qbuf[at, :], over_rows, preferred_element_type=F32)
            )
            places.append((blk, t))
        mine_rows = pl.ds(pl.multiple_of(replica * piece, piece), piece)
        for y in range(group):
            send_back(dq_send, piece, q_out, mine_rows, 0, i * group + y)
        scatter(got, places, dk_acc, dk_anchor, dk_chain)
        return _

    lax.fori_loop(0, steps, score_terms, 0)
    finish(dk_acc, dk_anchor, dk_chain, dk_send, k_out, 1)

    total = jnp.sum(temp_acc[...], axis=1, keepdims=True)
    total = jnp.sum(total, axis=0, keepdims=True) * reciprocal
    pair_terms[mine] = jnp.broadcast_to(total, (8, 128))
    for o in range(1, nf):
        pltpu.make_async_remote_copy(
            src_ref=pair_terms.at[mine],
            dst_ref=pair_terms.at[mine],
            send_sem=term_send.at[0],
            recv_sem=term_recv.at[0],
            device_id={"fsdp": (mine + o) % nf},
            device_id_type=MESH,
        ).start()
    rest = pair_terms.at[pl.ds(0, nf - 1)]
    pltpu.make_async_copy(rest, rest, term_recv.at[0]).wait()
    pltpu.make_async_copy(rest, rest, term_send.at[0]).wait()
    total = pair_terms[0]
    for o in range(1, nf):
        total += pair_terms[o]
    item_terms[me] = total

    def tell(o, _):
        pltpu.make_async_remote_copy(
            src_ref=item_terms.at[me],
            dst_ref=item_terms.at[me],
            send_sem=term_send.at[1],
            recv_sem=term_recv.at[1],
            device_id={"seq": (me + o) % n},
            device_id_type=MESH,
        ).start()
        return _

    lax.fori_loop(1, n, tell, 0)
    rest = item_terms.at[pl.ds(0, n - 1)]
    pltpu.make_async_copy(rest, rest, term_recv.at[1]).wait()
    pltpu.make_async_copy(rest, rest, term_send.at[1]).wait()
    lane = lax.broadcasted_iota(jnp.int32, (8, 128), 1)
    result = jnp.zeros((8, 128), F32)
    for d in range(n):
        result += jnp.where(lane == d // copies % heads, item_terms[d], 0.0)
    scale_out[...] = result

    sent(2)
    sent(3)
    for x, (source, rows, target) in enumerate(
        ((dq_send, piece, q_out), (dk_send, tok, k_out), (dv_send, tok, v_out))
    ):
        ref = source.at[pl.ds(0, (n - 1) * rows)]
        pltpu.make_async_copy(ref, ref, out_send.at[x]).wait()
        pltpu.make_async_copy(target, target, out_recv.at[x]).wait()


def hand_over(arrays, scales, heads):
    count, chunks = len(arrays), 4

    def kernel(*refs):
        sources, scale_ref = refs[:count], refs[count]
        targets, scale_out, sems = refs[count + 1 : -2], refs[-2], refs[-1]
        copies = []
        for x, (source, target) in enumerate(zip(sources, targets)):
            rows = source.shape[0] // chunks
            for y in range(chunks):
                at = pl.ds(y * rows, rows)
                copies.append(
                    pltpu.make_async_copy(source.at[at], target.at[at], sems.at[x * chunks + y])
                )
                copies[-1].start()
        scale_out[...] = scale_ref[0:1, :heads]
        for copy in copies:
            copy.wait()

    anywhere = pl.BlockSpec(memory_space=pl.ANY)
    local = pl.BlockSpec(memory_space=pltpu.VMEM)
    return pl.pallas_call(
        kernel,
        out_shape=[jax.ShapeDtypeStruct(a.shape, a.dtype) for a in arrays]
        + [jax.ShapeDtypeStruct((1, heads), F32)],
        in_specs=[anywhere] * count + [local],
        out_specs=[anywhere] * count + [local],
        scratch_shapes=[pltpu.SemaphoreType.DMA((count * chunks,))],
    )(*arrays, scales)


def slot_table(anchor_tiles, sampled_tiles, head, blocks, nblocks):
    tiles = jnp.take(lax.dynamic_index_in_dim(sampled_tiles, head, 0, False), blocks, axis=0)
    tiles = tiles.reshape(-1).astype(jnp.int32)
    place = jnp.arange(tiles.shape[0], dtype=jnp.int32)
    earlier = (tiles[:, None] == tiles[None, :]) & (place[None, :] < place[:, None])
    before = jnp.max(jnp.where(earlier, place[None, :] + 1, 0), axis=1)
    ids = jnp.arange(nblocks, dtype=jnp.int32)
    last = jnp.max(jnp.where(tiles[None, :] == ids[:, None], place[None, :] + 1, 0), axis=1)
    anchors = lax.dynamic_index_in_dim(anchor_tiles, head, 0, False).astype(jnp.int32)
    return jnp.concatenate([tiles, before, last, anchors])


def on_device(n, nf, probe, matcher, payload, adjoint, logit_scale, anchor_tiles, sampled_tiles):
    tok, seq_count, total_width = probe.shape
    heads = logit_scale.shape[0]
    width = total_width // heads
    copies = n // (seq_count * heads)
    assert seq_count == 1 and copies * heads == n
    piece = tok // copies
    tile = min(TILE_SPAN, piece)
    units = piece // tile
    n_anchor, n_random = anchor_tiles.shape[1], sampled_tiles.shape[2]
    nblocks = n * tok // TILE_SPAN
    me = lax.axis_index("seq")
    order = jnp.arange(n * units, dtype=jnp.int32)
    peer = (me + 1 + order // units) % n
    blocks = (peer * tok + me % copies * piece + order % units * tile) // TILE_SPAN
    table = slot_table(anchor_tiles, sampled_tiles, me // copies % heads, blocks, nblocks)

    dims = (n, nf, copies, tok, piece, tile, width, heads, n_anchor, n_random)
    keys = n * tok
    queries = n * piece
    slots = (3 + n_anchor + n_random) * TILE_SPAN
    chain = (n * units * n_random + 1, TILE_SPAN, width)
    padded = (nblocks + 2, TILE_SPAN, width)
    anywhere = pl.BlockSpec(memory_space=pl.ANY)
    scalars = pl.BlockSpec(memory_space=pltpu.SMEM)
    flat = lambda array: array.reshape(tok, total_width)
    tiled = lambda array: array.reshape(tok // TILE_SPAN, TILE_SPAN, total_width)
    parts = jax.ShapeDtypeStruct((tok, n * width), BF16)
    q_out, k_out, v_out, scales = pl.pallas_call(
        functools.partial(attention_kernel, dims),
        out_shape=(
            jax.ShapeDtypeStruct((tok, total_width), BF16),
            parts,
            parts,
            jax.ShapeDtypeStruct((8, 128), F32),
        ),
        in_specs=[anywhere] * 4 + [scalars] * 2,
        out_specs=(anywhere, anywhere, anywhere, pl.BlockSpec(memory_space=pltpu.VMEM)),
        scratch_shapes=[
            pltpu.VMEM((queries, width), BF16),
            pltpu.VMEM(padded, BF16),
            pltpu.VMEM(padded, BF16),
            pltpu.VMEM((queries, width), BF16),
            pltpu.VMEM((queries, slots), F32),
            pltpu.VMEM((queries, slots), F32),
            pltpu.VMEM(padded, F32),
            pltpu.VMEM(padded, F32),
            pltpu.VMEM((n_anchor, TILE_SPAN, width), F32),
            pltpu.VMEM((n_anchor, TILE_SPAN, width), F32),
            pltpu.VMEM(chain, F32),
            pltpu.VMEM(chain, F32),
            pltpu.VMEM((queries, width), BF16),
            pltpu.VMEM((keys, width), BF16),
            pltpu.VMEM((keys, width), BF16),
            pltpu.VMEM((8, 128), F32),
            pltpu.VMEM((nf, 8, 128), F32),
            pltpu.VMEM((n, 8, 128), F32),
            pltpu.SemaphoreType.DMA((4,)),
            pltpu.SemaphoreType.DMA((4,)),
            pltpu.SemaphoreType.DMA((3,)),
            pltpu.SemaphoreType.DMA((3,)),
            pltpu.SemaphoreType.DMA((2,)),
            pltpu.SemaphoreType.DMA((2,)),
        ],
        compiler_params=pltpu.CompilerParams(
            collective_id=0, has_side_effects=True, vmem_limit_bytes=56 * 1024 * 1024
        ),
        cost_estimate=pl.CostEstimate(
            flops=10 * queries * slots * width,
            bytes_accessed=14 * tok * total_width,
            transcendentals=queries * slots,
        ),
    )(flat(probe), tiled(matcher), tiled(payload), flat(adjoint), logit_scale, table)

    def combine(received):
        pieces = received.astype(F32).reshape(tok, heads, copies, width)
        return jnp.sum(pieces, axis=2).astype(BF16)

    if copies == 1:
        q_out, k_out, v_out, scales = hand_over((q_out, k_out, v_out), scales, heads)
    else:
        q_out, scales = hand_over((q_out,), scales, heads)
        k_out, v_out = combine(k_out), combine(v_out)
    shaped = lambda array: array.reshape(probe.shape)
    return shaped(q_out), shaped(k_out), shaped(v_out), scales.reshape(heads)


def solution(mesh):
    placed = P("seq", "fsdp", None)
    return jax.shard_map(
        functools.partial(on_device, mesh.shape["seq"], mesh.shape["fsdp"]),
        mesh=mesh,
        in_specs=(placed, placed, placed, placed, P(), P(), P()),
        out_specs=(placed, placed, placed, P()),
        check_vma=False,
    )
```

```python
import functools
import math

import jax
import jax.numpy as jnp
from jax import lax
from jax.experimental import pallas as pl
from jax.experimental.pallas import tpu as pltpu
from jax.sharding import PartitionSpec as P

TILE_SPAN = 64
STRIDE = 5
MASKED = -1e30
MESH = pl.DeviceIdType.MESH
F32 = jnp.float32
BF16 = jnp.bfloat16


def peer_of(me, i, n):
    stride = STRIDE if math.gcd(STRIDE, n) == 1 else 1
    return (me + i * stride) % n


def attention_kernel(
    dims,
    q_in,
    k_in,
    v_in,
    g_in,
    scale_in,
    table,
    q_out,
    k_out,
    v_out,
    scale_out,
    qbuf,
    kbuf,
    vbuf,
    gbuf,
    s_ref,
    p_ref,
    dk_acc,
    dv_acc,
    dk_anchor,
    dv_anchor,
    dk_chain,
    dv_chain,
    dq_send,
    dk_send,
    dv_send,
    temp_acc,
    pair_terms,
    item_terms,
    in_send,
    in_recv,
    out_send,
    out_recv,
    term_send,
    term_recv,
):
    n, nf, copies, tok, piece, tile, width, heads, n_anchor, n_random = dims
    span = TILE_SPAN
    nblocks = n * tok // span
    units = piece // tile
    entries = n * units * n_random
    window = 3 * span
    reciprocal = 1.0 / math.sqrt(width)
    me = lax.axis_index("seq")
    mine = lax.axis_index("fsdp")
    item = me // copies
    replica = me % copies
    cols = lambda d: pl.ds(pl.multiple_of(d // copies * width, width), width)

    barrier = pltpu.get_barrier_semaphore()

    def greet(o, _):
        pl.semaphore_signal(
            barrier, inc=1, device_id={"seq": (me + o) % n}, device_id_type=MESH
        )
        return _

    lax.fori_loop(1, n, greet, 0)
    for o in range(1, nf):
        pl.semaphore_signal(
            barrier, inc=1, device_id={"fsdp": (mine + o) % nf}, device_id_type=MESH
        )
    pl.semaphore_wait(barrier, n - 1 + nf - 1)

    arrivals = (
        (k_in, kbuf, tok // span, 1),
        (q_in, qbuf, piece, 0),
        (g_in, gbuf, piece, 0),
        (v_in, vbuf, tok // span, 1),
    )

    def prepare():
        zero_block = jnp.zeros((span, width), BF16)
        for buf in (kbuf, vbuf):
            buf[0] = zero_block
            buf[nblocks + 1] = zero_block

        def clear(c, _):
            dk_acc[c] = jnp.zeros((span, width), F32)
            dv_acc[c] = jnp.zeros((span, width), F32)
            return _

        lax.fori_loop(0, nblocks + 2, clear, 0)
        dk_anchor[...] = jnp.zeros_like(dk_anchor)
        dv_anchor[...] = jnp.zeros_like(dv_anchor)
        dk_chain[0] = jnp.zeros((span, width), F32)
        dv_chain[0] = jnp.zeros((span, width), F32)
        temp_acc[...] = jnp.zeros_like(temp_acc)

    def sent(a):
        _, target, rows, _ = arrivals[a]
        ref = target.at[pl.ds(0, (n - 1) * rows)]
        pltpu.make_async_copy(ref, ref, in_send.at[a]).wait()

    for a, (source, target, rows, shift) in enumerate(arrivals):
        if a == 2:
            prepare()
        if a >= 2:
            sent(a - 2)

        def block(d):
            if shift:
                return source.at[:, :, cols(d)]
            return source.at[pl.ds(pl.multiple_of(d % copies * rows, rows), rows), cols(d)]

        if shift:
            landing = target.at[pl.ds(shift + me * rows, rows)]
        else:
            landing = target.at[pl.ds(pl.multiple_of(me * rows, rows), rows)]

        def send(o, _):
            d = peer_of(me, o, n)
            pltpu.make_async_remote_copy(
                src_ref=block(d),
                dst_ref=landing,
                send_sem=in_send.at[a],
                recv_sem=in_recv.at[a],
                device_id={"seq": d},
                device_id_type=MESH,
            ).start()
            return _

        pltpu.make_async_copy(block(me), landing, in_recv.at[a]).start()
        lax.fori_loop(1, n, send, 0)

    def arrive(a):
        _, target, rows, shift = arrivals[a]
        ref = target.at[pl.ds(shift, n * rows)]
        pltpu.make_async_copy(ref, ref, in_recv.at[a]).wait()

    scale = scale_in[item % heads]
    alpha = scale * reciprocal
    anchors = [table[2 * entries + nblocks + x] for x in range(n_anchor)]
    slots = 3 + n_anchor + n_random
    slot_of = lax.broadcasted_iota(jnp.int32, (1, slots * span), 1) // span

    def unit_at(k, j):
        p = peer_of(me, k + 1, n)
        row = pl.multiple_of(p * piece + j * tile, tile)
        blk = (p * tok + replica * piece + j * tile) // span
        return pl.ds(row, tile), blk, k * units + j

    def select(buf, blk, t):
        parts = [buf[pl.ds(blk, 3)].reshape(window, width)]
        for a in anchors:
            parts.append(buf[a + 1])
        for x in range(n_random):
            parts.append(buf[table[t * n_random + x] + 1])
        return jnp.concatenate(parts, axis=0)

    def bias_of(blk):
        off = lambda dead: jnp.where(dead, MASKED, 0.0).astype(F32)
        bias = jnp.where(slot_of == 0, off(blk == 0), 0.0)
        bias = jnp.where(slot_of == 2, off(blk == nblocks - 1), bias)
        for x, a in enumerate(anchors):
            bias = jnp.where(slot_of == 3 + x, off(jnp.abs(a - blk) <= 1), bias)
        return bias

    def scatter(got, places, acc, anchor, chain):
        base = window + n_anchor * span
        for (blk, t), d in zip(places, got):
            acc[pl.ds(blk, 3)] += d[:window].reshape(3, span, width)
            anchor[...] += d[window:base].reshape(n_anchor, span, width)
            for x in range(n_random):
                e = t * n_random + x
                before = table[entries + e]
                chain[e + 1] = chain[before] + d[base + x * span : base + (x + 1) * span]

    rows_by_cols = (((1,), (1,)), ((), ()))
    over_rows = (((0,), (0,)), ((), ()))

    arrive(0)
    arrive(1)

    group = 2 if units <= 2 else 1
    steps = n // group
    members = lambda i: [(i * group + y, j) for y in range(group) for j in range(units)]

    def scores(i, _):
        for k, j in members(i):
            at, blk, t = unit_at(k, j)
            s = lax.dot_general(
                qbuf[at, :], select(kbuf, blk, t), rows_by_cols, preferred_element_type=F32
            )
            logits = s * alpha + bias_of(blk)
            e = jnp.exp(logits - jnp.max(logits, axis=1, keepdims=True))
            s_ref[at, :] = s
            p_ref[at, :] = e * (1.0 / jnp.sum(e, axis=1, keepdims=True))
        return _

    lax.fori_loop(0, steps, scores, 0)

    arrive(2)

    def value_terms(i, _):
        got, places = [], []
        for k, j in members(i):
            at, blk, t = unit_at(k, j)
            low = p_ref[at, :].astype(BF16)
            got.append(
                lax.dot_general(low, gbuf[at, :], over_rows, preferred_element_type=F32)
            )
            places.append((blk, t))
        scatter(got, places, dv_acc, dv_anchor, dv_chain)
        return _

    lax.fori_loop(0, steps, value_terms, 0)

    def send_back(source, rows, target, target_rows, x, k):
        d = peer_of(me, k + 1, n)
        block = source.at[pl.ds(pl.multiple_of(d * rows, rows), rows)]

        @pl.when(k < n - 1)
        def _():
            pltpu.make_async_remote_copy(
                src_ref=block,
                dst_ref=target.at[target_rows, landing_cols[x]],
                send_sem=out_send.at[x],
                recv_sem=out_recv.at[x],
                device_id={"seq": d},
                device_id_type=MESH,
            ).start()

        @pl.when(k == n - 1)
        def _():
            pltpu.make_async_copy(
                source.at[pl.ds(pl.multiple_of(me * rows, rows), rows)],
                target.at[target_rows, landing_cols[x]],
                out_recv.at[x],
            ).start()

    own_part = pl.ds(pl.multiple_of(me * width, width), width)
    landing_cols = (cols(me), own_part, own_part)

    def finish(acc, anchor, chain, source, target, x):
        def step(k, _):
            d = peer_of(me, k + 1, n)
            for b in range(tok // span):
                c = d * (tok // span) + b
                last = table[2 * entries + c]
                total = acc[c + 1] + chain[last]
                for y, a in enumerate(anchors):
                    total += jnp.where(a == c, anchor[y], 0.0)
                source[pl.ds(pl.multiple_of(c * span, span), span), :] = total.astype(BF16)
            send_back(source, tok, target, slice(None), x, k)
            return _

        lax.fori_loop(0, n, step, 0)

    finish(dv_acc, dv_anchor, dv_chain, dv_send, v_out, 2)

    arrive(3)

    def score_terms(i, _):
        got, places = [], []
        for k, j in members(i):
            at, blk, t = unit_at(k, j)
            dprob = lax.dot_general(
                gbuf[at, :], select(vbuf, blk, t), rows_by_cols, preferred_element_type=F32
            )
            prob = p_ref[at, :]
            delta = jnp.sum(prob * dprob, axis=1, keepdims=True)
            dscore = prob * (dprob - delta)
            both = dscore * s_ref[at, :]
            lanes = both[:, :width]
            for y in range(1, slots * span // width):
                lanes += both[:, y * width : (y + 1) * width]
            part = lanes[0:8]
            for y in range(1, tile // 8):
                part += lanes[y * 8 : (y + 1) * 8]
            temp_acc[...] += part
            draw = (dscore * alpha).astype(BF16)
            dq = jnp.dot(draw, select(kbuf, blk, t), preferred_element_type=F32)
            dq_send[at, :] = dq.astype(BF16)
            got.append(
                lax.dot_general(draw, qbuf[at, :], over_rows, preferred_element_type=F32)
            )
            places.append((blk, t))
        mine_rows = pl.ds(pl.multiple_of(replica * piece, piece), piece)
        for y in range(group):
            send_back(dq_send, piece, q_out, mine_rows, 0, i * group + y)
        scatter(got, places, dk_acc, dk_anchor, dk_chain)
        return _

    lax.fori_loop(0, steps, score_terms, 0)
    finish(dk_acc, dk_anchor, dk_chain, dk_send, k_out, 1)

    total = jnp.sum(temp_acc[...], axis=1, keepdims=True)
    total = jnp.sum(total, axis=0, keepdims=True) * reciprocal
    pair_terms[mine] = jnp.broadcast_to(total, (8, 128))
    for o in range(1, nf):
        pltpu.make_async_remote_copy(
            src_ref=pair_terms.at[mine],
            dst_ref=pair_terms.at[mine],
            send_sem=term_send.at[0],
            recv_sem=term_recv.at[0],
            device_id={"fsdp": (mine + o) % nf},
            device_id_type=MESH,
        ).start()
    rest = pair_terms.at[pl.ds(0, nf - 1)]
    pltpu.make_async_copy(rest, rest, term_recv.at[0]).wait()
    pltpu.make_async_copy(rest, rest, term_send.at[0]).wait()
    total = pair_terms[0]
    for o in range(1, nf):
        total += pair_terms[o]
    item_terms[me] = total

    def tell(o, _):
        pltpu.make_async_remote_copy(
            src_ref=item_terms.at[me],
            dst_ref=item_terms.at[me],
            send_sem=term_send.at[1],
            recv_sem=term_recv.at[1],
            device_id={"seq": (me + o) % n},
            device_id_type=MESH,
        ).start()
        return _

    lax.fori_loop(1, n, tell, 0)
    rest = item_terms.at[pl.ds(0, n - 1)]
    pltpu.make_async_copy(rest, rest, term_recv.at[1]).wait()
    pltpu.make_async_copy(rest, rest, term_send.at[1]).wait()
    lane = lax.broadcasted_iota(jnp.int32, (8, 128), 1)
    result = jnp.zeros((8, 128), F32)
    for d in range(n):
        result += jnp.where(lane == d // copies % heads, item_terms[d], 0.0)
    scale_out[...] = result

    sent(2)
    sent(3)
    for x, (source, rows, target) in enumerate(
        ((dq_send, piece, q_out), (dk_send, tok, k_out), (dv_send, tok, v_out))
    ):
        ref = source.at[pl.ds(0, (n - 1) * rows)]
        pltpu.make_async_copy(ref, ref, out_send.at[x]).wait()
        pltpu.make_async_copy(target, target, out_recv.at[x]).wait()


def hand_over(arrays, scales, heads):
    count = len(arrays)

    def kernel(*refs):
        sources, scale_ref = refs[:count], refs[count]
        targets, scale_out, sems = refs[count + 1 : -2], refs[-2], refs[-1]
        copies = []
        for x, (source, target) in enumerate(zip(sources, targets)):
            copies.append(pltpu.make_async_copy(source, target, sems.at[x]))
            copies[-1].start()
        scale_out[...] = scale_ref[0:1, :heads]
        for copy in copies:
            copy.wait()

    anywhere = pl.BlockSpec(memory_space=pl.ANY)
    local = pl.BlockSpec(memory_space=pltpu.VMEM)
    return pl.pallas_call(
        kernel,
        out_shape=[jax.ShapeDtypeStruct(a.shape, a.dtype) for a in arrays]
        + [jax.ShapeDtypeStruct((1, heads), F32)],
        in_specs=[local] * count + [local],
        out_specs=[anywhere] * count + [local],
        scratch_shapes=[pltpu.SemaphoreType.DMA((count,))],
    )(*arrays, scales)


def slot_table(anchor_tiles, sampled_tiles, head, blocks, nblocks):
    tiles = jnp.take(lax.dynamic_index_in_dim(sampled_tiles, head, 0, False), blocks, axis=0)
    tiles = tiles.reshape(-1).astype(jnp.int32)
    place = jnp.arange(tiles.shape[0], dtype=jnp.int32)
    earlier = (tiles[:, None] == tiles[None, :]) & (place[None, :] < place[:, None])
    before = jnp.max(jnp.where(earlier, place[None, :] + 1, 0), axis=1)
    ids = jnp.arange(nblocks, dtype=jnp.int32)
    last = jnp.max(jnp.where(tiles[None, :] == ids[:, None], place[None, :] + 1, 0), axis=1)
    anchors = lax.dynamic_index_in_dim(anchor_tiles, head, 0, False).astype(jnp.int32)
    return jnp.concatenate([tiles, before, last, anchors])


def on_device(n, nf, probe, matcher, payload, adjoint, logit_scale, anchor_tiles, sampled_tiles):
    tok, seq_count, total_width = probe.shape
    heads = logit_scale.shape[0]
    width = total_width // heads
    copies = n // (seq_count * heads)
    assert seq_count == 1 and copies * heads == n
    piece = tok // copies
    tile = min(TILE_SPAN, piece)
    units = piece // tile
    n_anchor, n_random = anchor_tiles.shape[1], sampled_tiles.shape[2]
    nblocks = n * tok // TILE_SPAN
    me = lax.axis_index("seq")
    order = jnp.arange(n * units, dtype=jnp.int32)
    peer = peer_of(me, order // units + 1, n)
    blocks = (peer * tok + me % copies * piece + order % units * tile) // TILE_SPAN
    table = slot_table(anchor_tiles, sampled_tiles, me // copies % heads, blocks, nblocks)

    dims = (n, nf, copies, tok, piece, tile, width, heads, n_anchor, n_random)
    keys = n * tok
    queries = n * piece
    slots = (3 + n_anchor + n_random) * TILE_SPAN
    chain = (n * units * n_random + 1, TILE_SPAN, width)
    padded = (nblocks + 2, TILE_SPAN, width)
    anywhere = pl.BlockSpec(memory_space=pl.ANY)
    scalars = pl.BlockSpec(memory_space=pltpu.SMEM)
    flat = lambda array: array.reshape(tok, total_width)
    tiled = lambda array: array.reshape(tok // TILE_SPAN, TILE_SPAN, total_width)
    parts = jax.ShapeDtypeStruct((tok, n * width), BF16)
    q_out, k_out, v_out, scales = pl.pallas_call(
        functools.partial(attention_kernel, dims),
        out_shape=(
            jax.ShapeDtypeStruct((tok, total_width), BF16),
            parts,
            parts,
            jax.ShapeDtypeStruct((8, 128), F32),
        ),
        in_specs=[anywhere] * 4 + [scalars] * 2,
        out_specs=(anywhere, anywhere, anywhere, pl.BlockSpec(memory_space=pltpu.VMEM)),
        scratch_shapes=[
            pltpu.VMEM((queries, width), BF16),
            pltpu.VMEM(padded, BF16),
            pltpu.VMEM(padded, BF16),
            pltpu.VMEM((queries, width), BF16),
            pltpu.VMEM((queries, slots), F32),
            pltpu.VMEM((queries, slots), F32),
            pltpu.VMEM(padded, F32),
            pltpu.VMEM(padded, F32),
            pltpu.VMEM((n_anchor, TILE_SPAN, width), F32),
            pltpu.VMEM((n_anchor, TILE_SPAN, width), F32),
            pltpu.VMEM(chain, F32),
            pltpu.VMEM(chain, F32),
            pltpu.VMEM((queries, width), BF16),
            pltpu.VMEM((keys, width), BF16),
            pltpu.VMEM((keys, width), BF16),
            pltpu.VMEM((8, 128), F32),
            pltpu.VMEM((nf, 8, 128), F32),
            pltpu.VMEM((n, 8, 128), F32),
            pltpu.SemaphoreType.DMA((4,)),
            pltpu.SemaphoreType.DMA((4,)),
            pltpu.SemaphoreType.DMA((3,)),
            pltpu.SemaphoreType.DMA((3,)),
            pltpu.SemaphoreType.DMA((2,)),
            pltpu.SemaphoreType.DMA((2,)),
        ],
        compiler_params=pltpu.CompilerParams(
            collective_id=0, has_side_effects=True, vmem_limit_bytes=56 * 1024 * 1024
        ),
        cost_estimate=pl.CostEstimate(
            flops=10 * queries * slots * width,
            bytes_accessed=14 * tok * total_width,
            transcendentals=queries * slots,
        ),
    )(flat(probe), tiled(matcher), tiled(payload), flat(adjoint), logit_scale, table)

    def combine(received):
        pieces = received.astype(F32).reshape(tok, heads, copies, width)
        return jnp.sum(pieces, axis=2).astype(BF16)

    if copies == 1:
        q_out, k_out, v_out, scales = hand_over((q_out, k_out, v_out), scales, heads)
    else:
        q_out, scales = hand_over((q_out,), scales, heads)
        k_out, v_out = combine(k_out), combine(v_out)
    shaped = lambda array: array.reshape(probe.shape)
    return shaped(q_out), shaped(k_out), shaped(v_out), scales.reshape(heads)


def solution(mesh):
    placed = P("seq", "fsdp", None)
    return jax.shard_map(
        functools.partial(on_device, mesh.shape["seq"], mesh.shape["fsdp"]),
        mesh=mesh,
        in_specs=(placed, placed, placed, placed, P(), P(), P()),
        out_specs=(placed, placed, placed, P()),
        check_vma=False,
    )
```

```python
import functools
import math

import jax
import jax.numpy as jnp
from jax import lax
from jax.experimental import pallas as pl
from jax.experimental.pallas import tpu as pltpu
from jax.sharding import PartitionSpec as P

TILE_SPAN = 64
STRIDE = 5
MASKED = -1e30
MESH = pl.DeviceIdType.MESH
F32 = jnp.float32
BF16 = jnp.bfloat16


def stride_of(n):
    return STRIDE if math.gcd(STRIDE, n) == 1 else 1


def peer_of(me, i, n):
    return (me + i * stride_of(n)) % n


def turn_of(me, peer, n):
    return ((peer - me + n) * pow(stride_of(n), -1, n) + n - 1) % n


def attention_kernel(
    dims,
    q_in,
    k_in,
    v_in,
    g_in,
    scale_in,
    table,
    q_out,
    k_out,
    v_out,
    scale_out,
    qbuf,
    kbuf,
    vbuf,
    gbuf,
    s_ref,
    p_ref,
    dk_acc,
    dv_acc,
    dk_anchor,
    dv_anchor,
    dk_chain,
    dv_chain,
    dq_send,
    dk_send,
    dv_send,
    temp_acc,
    pair_terms,
    item_terms,
    in_send,
    in_recv,
    out_send,
    out_recv,
    term_send,
    term_recv,
):
    n, nf, copies, tok, piece, tile, width, heads, n_anchor, n_random = dims
    span = TILE_SPAN
    nblocks = n * tok // span
    units = piece // tile
    entries = n * units * n_random
    window = 3 * span
    reciprocal = 1.0 / math.sqrt(width)
    me = lax.axis_index("seq")
    mine = lax.axis_index("fsdp")
    item = me // copies
    replica = me % copies
    cols = lambda d: pl.ds(pl.multiple_of(d // copies * width, width), width)

    barrier = pltpu.get_barrier_semaphore()

    def greet(o, _):
        pl.semaphore_signal(
            barrier, inc=1, device_id={"seq": (me + o) % n}, device_id_type=MESH
        )
        return _

    lax.fori_loop(1, n, greet, 0)
    for o in range(1, nf):
        pl.semaphore_signal(
            barrier, inc=1, device_id={"fsdp": (mine + o) % nf}, device_id_type=MESH
        )
    pl.semaphore_wait(barrier, n - 1 + nf - 1)

    arrivals = (
        (k_in, kbuf, tok // span, 1),
        (q_in, qbuf, piece, 0),
        (g_in, gbuf, piece, 0),
        (v_in, vbuf, tok // span, 1),
    )

    def prepare():
        zero_block = jnp.zeros((span, width), BF16)
        for buf in (kbuf, vbuf):
            buf[0] = zero_block
            buf[nblocks + 1] = zero_block

        def clear(c, _):
            dk_acc[c] = jnp.zeros((span, width), F32)
            dv_acc[c] = jnp.zeros((span, width), F32)
            return _

        lax.fori_loop(0, nblocks + 2, clear, 0)
        dk_anchor[...] = jnp.zeros_like(dk_anchor)
        dv_anchor[...] = jnp.zeros_like(dv_anchor)
        dk_chain[0] = jnp.zeros((span, width), F32)
        dv_chain[0] = jnp.zeros((span, width), F32)
        temp_acc[...] = jnp.zeros_like(temp_acc)

    def sent(a):
        _, target, rows, _ = arrivals[a]
        ref = target.at[pl.ds(0, (n - 1) * rows)]
        pltpu.make_async_copy(ref, ref, in_send.at[a]).wait()

    for a, (source, target, rows, shift) in enumerate(arrivals):
        if a == 2:
            prepare()
        if a >= 2:
            sent(a - 2)

        def block(d):
            if shift:
                return source.at[:, :, cols(d)]
            return source.at[pl.ds(pl.multiple_of(d % copies * rows, rows), rows), cols(d)]

        if shift:
            landing = target.at[pl.ds(shift + me * rows, rows)]
        else:
            landing = target.at[pl.ds(pl.multiple_of(me * rows, rows), rows)]

        def send(o, _):
            d = peer_of(me, o, n)
            pltpu.make_async_remote_copy(
                src_ref=block(d),
                dst_ref=landing,
                send_sem=in_send.at[a],
                recv_sem=in_recv.at[a],
                device_id={"seq": d},
                device_id_type=MESH,
            ).start()
            return _

        pltpu.make_async_copy(block(me), landing, in_recv.at[a]).start()
        lax.fori_loop(1, n, send, 0)

    def arrive(a):
        _, target, rows, shift = arrivals[a]
        ref = target.at[pl.ds(shift, n * rows)]
        pltpu.make_async_copy(ref, ref, in_recv.at[a]).wait()

    scale = scale_in[item % heads]
    alpha = scale * reciprocal
    anchors = [table[2 * entries + nblocks + x] for x in range(n_anchor)]
    slots = 3 + n_anchor + n_random
    slot_of = lax.broadcasted_iota(jnp.int32, (1, slots * span), 1) // span

    def unit_at(k, j):
        p = peer_of(me, k + 1, n)
        row = pl.multiple_of(p * piece + j * tile, tile)
        blk = (p * tok + replica * piece + j * tile) // span
        return pl.ds(row, tile), blk, (k * units + j, p * units + j)

    def select(buf, blk, t):
        parts = [buf[pl.ds(blk, 3)].reshape(window, width)]
        for a in anchors:
            parts.append(buf[a + 1])
        for x in range(n_random):
            parts.append(buf[table[t[1] * n_random + x] + 1])
        return jnp.concatenate(parts, axis=0)

    def bias_of(blk):
        off = lambda dead: jnp.where(dead, MASKED, 0.0).astype(F32)
        bias = jnp.where(slot_of == 0, off(blk == 0), 0.0)
        bias = jnp.where(slot_of == 2, off(blk == nblocks - 1), bias)
        for x, a in enumerate(anchors):
            bias = jnp.where(slot_of == 3 + x, off(jnp.abs(a - blk) <= 1), bias)
        return bias

    def scatter(d, blk, t, acc, anchor, chain):
        base = window + n_anchor * span
        acc[pl.ds(blk, 3)] += d[:window].reshape(3, span, width)
        anchor[...] += d[window:base].reshape(n_anchor, span, width)
        for x in range(n_random):
            before = table[entries + t[1] * n_random + x]
            chain[t[0] * n_random + x + 1] = (
                chain[before] + d[base + x * span : base + (x + 1) * span]
            )

    rows_by_cols = (((1,), (1,)), ((), ()))
    over_rows = (((0,), (0,)), ((), ()))

    arrive(0)
    arrive(1)

    group = 2 if units <= 2 else 1
    steps = n // group
    members = lambda i: [(i * group + y, j) for y in range(group) for j in range(units)]

    def scores(i, _):
        for k, j in members(i):
            at, blk, t = unit_at(k, j)
            s = lax.dot_general(
                qbuf[at, :], select(kbuf, blk, t), rows_by_cols, preferred_element_type=F32
            )
            logits = s * alpha + bias_of(blk)
            e = jnp.exp(logits - jnp.max(logits, axis=1, keepdims=True))
            s_ref[at, :] = s
            p_ref[at, :] = e * (1.0 / jnp.sum(e, axis=1, keepdims=True))
        return _

    lax.fori_loop(0, steps, scores, 0)

    arrive(2)

    def value_terms(i, _):
        for k, j in members(i):
            at, blk, t = unit_at(k, j)
            low = p_ref[at, :].astype(BF16)
            dv = lax.dot_general(low, gbuf[at, :], over_rows, preferred_element_type=F32)
            scatter(dv, blk, t, dv_acc, dv_anchor, dv_chain)
        return _

    lax.fori_loop(0, steps, value_terms, 0)

    def send_back(source, rows, target, target_rows, x, k):
        d = peer_of(me, k + 1, n)
        block = source.at[pl.ds(pl.multiple_of(d * rows, rows), rows)]

        @pl.when(k < n - 1)
        def _():
            pltpu.make_async_remote_copy(
                src_ref=block,
                dst_ref=target.at[target_rows, landing_cols[x]],
                send_sem=out_send.at[x],
                recv_sem=out_recv.at[x],
                device_id={"seq": d},
                device_id_type=MESH,
            ).start()

        @pl.when(k == n - 1)
        def _():
            pltpu.make_async_copy(
                source.at[pl.ds(pl.multiple_of(me * rows, rows), rows)],
                target.at[target_rows, landing_cols[x]],
                out_recv.at[x],
            ).start()

    own_part = pl.ds(pl.multiple_of(me * width, width), width)
    landing_cols = (cols(me), own_part, own_part)

    def finish(acc, anchor, chain, source, target, x):
        def step(k, _):
            d = peer_of(me, k + 1, n)
            for b in range(tok // span):
                c = d * (tok // span) + b
                last = table[2 * entries + c]
                total = acc[c + 1] + chain[last]
                for y, a in enumerate(anchors):
                    total += jnp.where(a == c, anchor[y], 0.0)
                source[pl.ds(pl.multiple_of(c * span, span), span), :] = total.astype(BF16)
            send_back(source, tok, target, slice(None), x, k)
            return _

        lax.fori_loop(0, n, step, 0)

    finish(dv_acc, dv_anchor, dv_chain, dv_send, v_out, 2)

    arrive(3)

    def score_terms(i, _):
        for k, j in members(i):
            at, blk, t = unit_at(k, j)
            dprob = lax.dot_general(
                gbuf[at, :], select(vbuf, blk, t), rows_by_cols, preferred_element_type=F32
            )
            prob = p_ref[at, :]
            delta = jnp.sum(prob * dprob, axis=1, keepdims=True)
            dscore = prob * (dprob - delta)
            both = dscore * s_ref[at, :]
            lanes = both[:, :width]
            for y in range(1, slots * span // width):
                lanes += both[:, y * width : (y + 1) * width]
            part = lanes[0:8]
            for y in range(1, tile // 8):
                part += lanes[y * 8 : (y + 1) * 8]
            temp_acc[...] += part
            draw = (dscore * alpha).astype(BF16)
            dq = jnp.dot(draw, select(kbuf, blk, t), preferred_element_type=F32)
            dq_send[at, :] = dq.astype(BF16)
            dk = lax.dot_general(draw, qbuf[at, :], over_rows, preferred_element_type=F32)
            scatter(dk, blk, t, dk_acc, dk_anchor, dk_chain)
        mine_rows = pl.ds(pl.multiple_of(replica * piece, piece), piece)
        for y in range(group):
            send_back(dq_send, piece, q_out, mine_rows, 0, i * group + y)
        return _

    lax.fori_loop(0, steps, score_terms, 0)
    finish(dk_acc, dk_anchor, dk_chain, dk_send, k_out, 1)

    total = jnp.sum(temp_acc[...], axis=1, keepdims=True)
    total = jnp.sum(total, axis=0, keepdims=True) * reciprocal
    pair_terms[mine] = jnp.broadcast_to(total, (8, 128))
    for o in range(1, nf):
        pltpu.make_async_remote_copy(
            src_ref=pair_terms.at[mine],
            dst_ref=pair_terms.at[mine],
            send_sem=term_send.at[0],
            recv_sem=term_recv.at[0],
            device_id={"fsdp": (mine + o) % nf},
            device_id_type=MESH,
        ).start()
    rest = pair_terms.at[pl.ds(0, nf - 1)]
    pltpu.make_async_copy(rest, rest, term_recv.at[0]).wait()
    pltpu.make_async_copy(rest, rest, term_send.at[0]).wait()
    total = pair_terms[0]
    for o in range(1, nf):
        total += pair_terms[o]
    item_terms[me] = total

    def tell(o, _):
        pltpu.make_async_remote_copy(
            src_ref=item_terms.at[me],
            dst_ref=item_terms.at[me],
            send_sem=term_send.at[1],
            recv_sem=term_recv.at[1],
            device_id={"seq": (me + o) % n},
            device_id_type=MESH,
        ).start()
        return _

    lax.fori_loop(1, n, tell, 0)
    rest = item_terms.at[pl.ds(0, n - 1)]
    pltpu.make_async_copy(rest, rest, term_recv.at[1]).wait()
    pltpu.make_async_copy(rest, rest, term_send.at[1]).wait()
    lane = lax.broadcasted_iota(jnp.int32, (8, 128), 1)
    result = jnp.zeros((8, 128), F32)
    for d in range(n):
        result += jnp.where(lane == d // copies % heads, item_terms[d], 0.0)
    scale_out[...] = result

    sent(2)
    sent(3)
    for x, (source, rows, target) in enumerate(
        ((dq_send, piece, q_out), (dk_send, tok, k_out), (dv_send, tok, v_out))
    ):
        ref = source.at[pl.ds(0, (n - 1) * rows)]
        pltpu.make_async_copy(ref, ref, out_send.at[x]).wait()
        pltpu.make_async_copy(target, target, out_recv.at[x]).wait()


def hand_over(arrays, scales, heads):
    count, halves = len(arrays), 2
    tok, total_width = arrays[0].shape
    rows = tok // halves

    def kernel(*refs):
        sources, scale_ref = refs[:count], refs[count]
        targets, scale_out = refs[count + 1 : -4], refs[-4]
        held, arrived, left = refs[-3:]
        pieces = [(x, y, pl.ds(y * rows, rows)) for x in range(count) for y in range(halves)]
        ins = [
            pltpu.make_async_copy(sources[x].at[at], held.at[x, at], arrived.at[x, y])
            for x, y, at in pieces
        ]
        outs = [
            pltpu.make_async_copy(held.at[x, at], targets[x].at[at], left.at[x, y])
            for x, y, at in pieces
        ]
        for copy in ins:
            copy.start()
        scale_out[...] = scale_ref[0:1, :heads]
        for first, second in zip(ins, outs):
            first.wait()
            second.start()
        for copy in outs:
            copy.wait()

    anywhere = pl.BlockSpec(memory_space=pl.ANY)
    local = pl.BlockSpec(memory_space=pltpu.VMEM)
    return pl.pallas_call(
        kernel,
        out_shape=[jax.ShapeDtypeStruct(a.shape, a.dtype) for a in arrays]
        + [jax.ShapeDtypeStruct((1, heads), F32)],
        in_specs=[anywhere] * count + [local],
        out_specs=[anywhere] * count + [local],
        scratch_shapes=[
            pltpu.VMEM((count, tok, total_width), BF16),
            pltpu.SemaphoreType.DMA((count, halves)),
            pltpu.SemaphoreType.DMA((count, halves)),
        ],
    )(*arrays, scales)


def slot_table(anchors, tiles, order, nblocks):
    tiles = tiles.astype(jnp.int32)
    place = order[:, None] * tiles.shape[1] + jnp.arange(tiles.shape[1], dtype=jnp.int32)
    tiles, place = tiles.reshape(-1), place.reshape(-1)
    earlier = (tiles[:, None] == tiles[None, :]) & (place[None, :] < place[:, None])
    before = jnp.max(jnp.where(earlier, place[None, :] + 1, 0), axis=1)
    ids = jnp.arange(nblocks, dtype=jnp.int32)
    last = jnp.max(jnp.where(tiles[None, :] == ids[:, None], place[None, :] + 1, 0), axis=1)
    return jnp.concatenate([tiles, before, last, anchors.astype(jnp.int32)])


def on_device(n, nf, probe, matcher, payload, adjoint, logit_scale, anchor_tiles, sampled_tiles):
    tok, seq_count, total_width = probe.shape
    heads = logit_scale.shape[0]
    width = total_width // heads
    copies = n // (seq_count * heads)
    assert seq_count == 1 and copies * heads == n
    piece = tok // copies
    tile = min(TILE_SPAN, piece)
    units = piece // tile
    n_anchor, n_random = anchor_tiles.shape[1], sampled_tiles.shape[2]
    nblocks = n * tok // TILE_SPAN
    me = lax.axis_index("seq")
    head = me // copies % heads
    unit = jnp.arange(n * units, dtype=jnp.int32)
    order = turn_of(me, unit // units, n) * units + unit % units
    tiles = lax.dynamic_index_in_dim(sampled_tiles, head, 0, False)
    anchors = lax.dynamic_index_in_dim(anchor_tiles, head, 0, False)
    if copies > 1:
        blocks = (unit // units * tok + me % copies * piece + unit % units * tile) // TILE_SPAN
        tiles = jnp.take(tiles, blocks, axis=0)
    table = slot_table(anchors, tiles, order, nblocks)

    dims = (n, nf, copies, tok, piece, tile, width, heads, n_anchor, n_random)
    keys = n * tok
    queries = n * piece
    slots = (3 + n_anchor + n_random) * TILE_SPAN
    chain = (n * units * n_random + 1, TILE_SPAN, width)
    padded = (nblocks + 2, TILE_SPAN, width)
    anywhere = pl.BlockSpec(memory_space=pl.ANY)
    scalars = pl.BlockSpec(memory_space=pltpu.SMEM)
    flat = lambda array: array.reshape(tok, total_width)
    tiled = lambda array: array.reshape(tok // TILE_SPAN, TILE_SPAN, total_width)
    parts = jax.ShapeDtypeStruct((tok, n * width), BF16)
    q_out, k_out, v_out, scales = pl.pallas_call(
        functools.partial(attention_kernel, dims),
        out_shape=(
            jax.ShapeDtypeStruct((tok, total_width), BF16),
            parts,
            parts,
            jax.ShapeDtypeStruct((8, 128), F32),
        ),
        in_specs=[anywhere] * 4 + [scalars] * 2,
        out_specs=(anywhere, anywhere, anywhere, pl.BlockSpec(memory_space=pltpu.VMEM)),
        scratch_shapes=[
            pltpu.VMEM((queries, width), BF16),
            pltpu.VMEM(padded, BF16),
            pltpu.VMEM(padded, BF16),
            pltpu.VMEM((queries, width), BF16),
            pltpu.VMEM((queries, slots), F32),
            pltpu.VMEM((queries, slots), F32),
            pltpu.VMEM(padded, F32),
            pltpu.VMEM(padded, F32),
            pltpu.VMEM((n_anchor, TILE_SPAN, width), F32),
            pltpu.VMEM((n_anchor, TILE_SPAN, width), F32),
            pltpu.VMEM(chain, F32),
            pltpu.VMEM(chain, F32),
            pltpu.VMEM((queries, width), BF16),
            pltpu.VMEM((keys, width), BF16),
            pltpu.VMEM((keys, width), BF16),
            pltpu.VMEM((8, 128), F32),
            pltpu.VMEM((nf, 8, 128), F32),
            pltpu.VMEM((n, 8, 128), F32),
            pltpu.SemaphoreType.DMA((4,)),
            pltpu.SemaphoreType.DMA((4,)),
            pltpu.SemaphoreType.DMA((3,)),
            pltpu.SemaphoreType.DMA((3,)),
            pltpu.SemaphoreType.DMA((2,)),
            pltpu.SemaphoreType.DMA((2,)),
        ],
        compiler_params=pltpu.CompilerParams(
            collective_id=0, has_side_effects=True, vmem_limit_bytes=56 * 1024 * 1024
        ),
        cost_estimate=pl.CostEstimate(
            flops=10 * queries * slots * width,
            bytes_accessed=14 * tok * total_width,
            transcendentals=queries * slots,
        ),
    )(flat(probe), tiled(matcher), tiled(payload), flat(adjoint), logit_scale, table)

    def combine(received):
        pieces = received.astype(F32).reshape(tok, heads, copies, width)
        return jnp.sum(pieces, axis=2).astype(BF16)

    if copies == 1:
        q_out, k_out, v_out, scales = hand_over((q_out, k_out, v_out), scales, heads)
    else:
        q_out, scales = hand_over((q_out,), scales, heads)
        k_out, v_out = combine(k_out), combine(v_out)
    shaped = lambda array: array.reshape(probe.shape)
    return shaped(q_out), shaped(k_out), shaped(v_out), scales.reshape(heads)


def solution(mesh):
    placed = P("seq", "fsdp", None)
    return jax.shard_map(
        functools.partial(on_device, mesh.shape["seq"], mesh.shape["fsdp"]),
        mesh=mesh,
        in_specs=(placed, placed, placed, placed, P(), P(), P()),
        out_specs=(placed, placed, placed, P()),
        check_vma=False,
    )
```

```python
import functools
import math

import jax
import jax.numpy as jnp
from jax import lax
from jax.experimental import pallas as pl
from jax.experimental.pallas import tpu as pltpu
from jax.sharding import PartitionSpec as P

TILE_SPAN = 64
STRIDE = 5
MASKED = -1e30
MESH = pl.DeviceIdType.MESH
F32 = jnp.float32
BF16 = jnp.bfloat16


def stride_of(n):
    return STRIDE if math.gcd(STRIDE, n) == 1 else 1


def peer_of(me, i, n):
    return (me + i * stride_of(n)) % n


def turn_of(me, peer, n):
    return ((peer - me + n) * pow(stride_of(n), -1, n) + n - 1) % n


def attention_kernel(
    dims,
    q_in,
    k_in,
    v_in,
    g_in,
    scale_in,
    table,
    q_out,
    k_out,
    v_out,
    scale_out,
    qbuf,
    kbuf,
    vbuf,
    gbuf,
    s_ref,
    p_ref,
    dk_acc,
    dv_acc,
    dk_anchor,
    dv_anchor,
    dk_chain,
    dv_chain,
    dq_send,
    dk_send,
    dv_send,
    temp_acc,
    pair_terms,
    item_terms,
    in_send,
    in_recv,
    out_send,
    out_recv,
    term_send,
    term_recv,
):
    n, nf, copies, tok, piece, tile, width, heads, n_anchor, n_random = dims
    span = TILE_SPAN
    nblocks = n * tok // span
    units = piece // tile
    entries = n * units * n_random
    window = 3 * span
    reciprocal = 1.0 / math.sqrt(width)
    me = lax.axis_index("seq")
    mine = lax.axis_index("fsdp")
    item = me // copies
    replica = me % copies
    cols = lambda d: pl.ds(pl.multiple_of(d // copies * width, width), width)

    barrier = pltpu.get_barrier_semaphore()

    def greet(o, _):
        pl.semaphore_signal(
            barrier, inc=1, device_id={"seq": (me + o) % n}, device_id_type=MESH
        )
        return _

    lax.fori_loop(1, n, greet, 0)
    for o in range(1, nf):
        pl.semaphore_signal(
            barrier, inc=1, device_id={"fsdp": (mine + o) % nf}, device_id_type=MESH
        )
    pl.semaphore_wait(barrier, n - 1 + nf - 1)

    arrivals = (
        (k_in, kbuf, tok // span, 1),
        (q_in, qbuf, piece, 0),
        (g_in, gbuf, piece, 0),
        (v_in, vbuf, tok // span, 1),
    )

    def prepare():
        zero_block = jnp.zeros((span, width), BF16)
        for buf in (kbuf, vbuf):
            buf[0] = zero_block
            buf[nblocks + 1] = zero_block

        def clear(c, _):
            dk_acc[c] = jnp.zeros((span, width), F32)
            dv_acc[c] = jnp.zeros((span, width), F32)
            return _

        lax.fori_loop(0, nblocks + 2, clear, 0)
        dk_anchor[...] = jnp.zeros_like(dk_anchor)
        dv_anchor[...] = jnp.zeros_like(dv_anchor)
        dk_chain[0] = jnp.zeros((span, width), F32)
        dv_chain[0] = jnp.zeros((span, width), F32)
        temp_acc[...] = jnp.zeros_like(temp_acc)

    def sent(a):
        _, target, rows, _ = arrivals[a]
        ref = target.at[pl.ds(0, (n - 1) * rows)]
        pltpu.make_async_copy(ref, ref, in_send.at[a]).wait()

    for a, (source, target, rows, shift) in enumerate(arrivals):
        if a == 2:
            prepare()
        if a >= 2:
            sent(a - 2)

        def block(d):
            if shift:
                return source.at[:, :, cols(d)]
            return source.at[pl.ds(pl.multiple_of(d % copies * rows, rows), rows), cols(d)]

        if shift:
            landing = target.at[pl.ds(shift + me * rows, rows)]
        else:
            landing = target.at[pl.ds(pl.multiple_of(me * rows, rows), rows)]

        def send(o, _):
            d = peer_of(me, o, n)
            pltpu.make_async_remote_copy(
                src_ref=block(d),
                dst_ref=landing,
                send_sem=in_send.at[a],
                recv_sem=in_recv.at[a],
                device_id={"seq": d},
                device_id_type=MESH,
            ).start()
            return _

        pltpu.make_async_copy(block(me), landing, in_recv.at[a]).start()
        lax.fori_loop(1, n, send, 0)

    def arrive(a):
        _, target, rows, shift = arrivals[a]
        ref = target.at[pl.ds(shift, n * rows)]
        pltpu.make_async_copy(ref, ref, in_recv.at[a]).wait()

    scale = scale_in[item % heads]
    alpha = scale * reciprocal
    anchors = [table[2 * entries + nblocks + x] for x in range(n_anchor)]
    slots = 3 + n_anchor + n_random
    slot_of = lax.broadcasted_iota(jnp.int32, (1, slots * span), 1) // span

    def unit_at(k, j):
        p = peer_of(me, k + 1, n)
        row = pl.multiple_of(p * piece + j * tile, tile)
        blk = (p * tok + replica * piece + j * tile) // span
        return pl.ds(row, tile), blk, (k * units + j, p * units + j)

    def select(buf, blk, t):
        parts = [buf[pl.ds(blk, 3)].reshape(window, width)]
        for a in anchors:
            parts.append(buf[a + 1])
        for x in range(n_random):
            parts.append(buf[table[t[1] * n_random + x] + 1])
        return jnp.concatenate(parts, axis=0)

    def bias_of(blk):
        off = lambda dead: jnp.where(dead, MASKED, 0.0).astype(F32)
        bias = jnp.where(slot_of == 0, off(blk == 0), 0.0)
        bias = jnp.where(slot_of == 2, off(blk == nblocks - 1), bias)
        for x, a in enumerate(anchors):
            bias = jnp.where(slot_of == 3 + x, off(jnp.abs(a - blk) <= 1), bias)
        return bias

    def scatter(d, blk, t, acc, anchor, chain):
        base = window + n_anchor * span
        acc[pl.ds(blk, 3)] += d[:window].reshape(3, span, width)
        anchor[...] += d[window:base].reshape(n_anchor, span, width)
        for x in range(n_random):
            before = table[entries + t[1] * n_random + x]
            chain[t[0] * n_random + x + 1] = (
                chain[before] + d[base + x * span : base + (x + 1) * span]
            )

    rows_by_cols = (((1,), (1,)), ((), ()))
    over_rows = (((0,), (0,)), ((), ()))

    arrive(0)
    arrive(1)

    group = 2 if units <= 2 else 1
    steps = n // group
    members = lambda i: [(i * group + y, j) for y in range(group) for j in range(units)]

    def scores(i, _):
        for k, j in members(i):
            at, blk, t = unit_at(k, j)
            s = lax.dot_general(
                qbuf[at, :], select(kbuf, blk, t), rows_by_cols, preferred_element_type=F32
            )
            logits = s * alpha + bias_of(blk)
            e = jnp.exp(logits - jnp.max(logits, axis=1, keepdims=True))
            s_ref[at, :] = s
            p_ref[at, :] = e * (1.0 / jnp.sum(e, axis=1, keepdims=True))
        return _

    lax.fori_loop(0, steps, scores, 0)

    arrive(2)

    def value_terms(i, _):
        for k, j in members(i):
            at, blk, t = unit_at(k, j)
            low = p_ref[at, :].astype(BF16)
            dv = lax.dot_general(low, gbuf[at, :], over_rows, preferred_element_type=F32)
            scatter(dv, blk, t, dv_acc, dv_anchor, dv_chain)
        return _

    lax.fori_loop(0, steps, value_terms, 0)

    def send_back(source, rows, target, target_rows, x, k):
        d = peer_of(me, k + 1, n)
        block = source.at[pl.ds(pl.multiple_of(d * rows, rows), rows)]

        @pl.when(k < n - 1)
        def _():
            pltpu.make_async_remote_copy(
                src_ref=block,
                dst_ref=target.at[target_rows, landing_cols[x]],
                send_sem=out_send.at[x],
                recv_sem=out_recv.at[x],
                device_id={"seq": d},
                device_id_type=MESH,
            ).start()

        @pl.when(k == n - 1)
        def _():
            pltpu.make_async_copy(
                source.at[pl.ds(pl.multiple_of(me * rows, rows), rows)],
                target.at[target_rows, landing_cols[x]],
                out_recv.at[x],
            ).start()

    own_part = pl.ds(pl.multiple_of(me * width, width), width)
    landing_cols = (cols(me), own_part, own_part)

    def finish(acc, anchor, chain, source, target, x):
        def step(k, _):
            d = peer_of(me, k + 1, n)
            for b in range(tok // span):
                c = d * (tok // span) + b
                last = table[2 * entries + c]
                total = acc[c + 1] + chain[last]
                for y, a in enumerate(anchors):
                    total += jnp.where(a == c, anchor[y], 0.0)
                source[pl.ds(pl.multiple_of(c * span, span), span), :] = total.astype(BF16)
            send_back(source, tok, target, slice(None), x, k)
            return _

        lax.fori_loop(0, n, step, 0)

    finish(dv_acc, dv_anchor, dv_chain, dv_send, v_out, 2)

    arrive(3)

    def score_terms(i, _):
        for k, j in members(i):
            at, blk, t = unit_at(k, j)
            dprob = lax.dot_general(
                gbuf[at, :], select(vbuf, blk, t), rows_by_cols, preferred_element_type=F32
            )
            prob = p_ref[at, :]
            delta = jnp.sum(prob * dprob, axis=1, keepdims=True)
            dscore = prob * (dprob - delta)
            both = dscore * s_ref[at, :]
            lanes = both[:, :width]
            for y in range(1, slots * span // width):
                lanes += both[:, y * width : (y + 1) * width]
            part = lanes[0:8]
            for y in range(1, tile // 8):
                part += lanes[y * 8 : (y + 1) * 8]
            temp_acc[...] += part
            draw = (dscore * alpha).astype(BF16)
            dq = jnp.dot(draw, select(kbuf, blk, t), preferred_element_type=F32)
            dq_send[at, :] = dq.astype(BF16)
            dk = lax.dot_general(draw, qbuf[at, :], over_rows, preferred_element_type=F32)
            scatter(dk, blk, t, dk_acc, dk_anchor, dk_chain)
        mine_rows = pl.ds(pl.multiple_of(replica * piece, piece), piece)
        for y in range(group):
            send_back(dq_send, piece, q_out, mine_rows, 0, i * group + y)
        return _

    lax.fori_loop(0, steps, score_terms, 0)
    finish(dk_acc, dk_anchor, dk_chain, dk_send, k_out, 1)

    total = jnp.sum(temp_acc[...], axis=1, keepdims=True)
    total = jnp.sum(total, axis=0, keepdims=True) * reciprocal
    pair_terms[mine] = jnp.broadcast_to(total, (8, 128))
    for o in range(1, nf):
        pltpu.make_async_remote_copy(
            src_ref=pair_terms.at[mine],
            dst_ref=pair_terms.at[mine],
            send_sem=term_send.at[0],
            recv_sem=term_recv.at[0],
            device_id={"fsdp": (mine + o) % nf},
            device_id_type=MESH,
        ).start()
    rest = pair_terms.at[pl.ds(0, nf - 1)]
    pltpu.make_async_copy(rest, rest, term_recv.at[0]).wait()
    pltpu.make_async_copy(rest, rest, term_send.at[0]).wait()
    total = pair_terms[0]
    for o in range(1, nf):
        total += pair_terms[o]
    item_terms[me] = total

    def tell(o, _):
        pltpu.make_async_remote_copy(
            src_ref=item_terms.at[me],
            dst_ref=item_terms.at[me],
            send_sem=term_send.at[1],
            recv_sem=term_recv.at[1],
            device_id={"seq": (me + o) % n},
            device_id_type=MESH,
        ).start()
        return _

    lax.fori_loop(1, n, tell, 0)
    rest = item_terms.at[pl.ds(0, n - 1)]
    pltpu.make_async_copy(rest, rest, term_recv.at[1]).wait()
    pltpu.make_async_copy(rest, rest, term_send.at[1]).wait()
    lane = lax.broadcasted_iota(jnp.int32, (8, 128), 1)
    result = jnp.zeros((8, 128), F32)
    for d in range(n):
        result += jnp.where(lane == d // copies % heads, item_terms[d], 0.0)
    scale_out[...] = result

    sent(2)
    sent(3)
    for x, (source, rows, target) in enumerate(
        ((dq_send, piece, q_out), (dk_send, tok, k_out), (dv_send, tok, v_out))
    ):
        ref = source.at[pl.ds(0, (n - 1) * rows)]
        pltpu.make_async_copy(ref, ref, out_send.at[x]).wait()
        pltpu.make_async_copy(target, target, out_recv.at[x]).wait()


def hand_over(arrays, scales, heads):
    count = len(arrays)

    def kernel(*refs):
        sources, scale_ref = refs[:count], refs[count]
        targets, scale_out, sems = refs[count + 1 : -2], refs[-2], refs[-1]
        copies = []
        for x, (source, target) in enumerate(zip(sources, targets)):
            copies.append(pltpu.make_async_copy(source, target, sems.at[x]))
            copies[-1].start()
        scale_out[...] = scale_ref[0:1, :heads]
        for copy in copies:
            copy.wait()

    anywhere = pl.BlockSpec(memory_space=pl.ANY)
    local = pl.BlockSpec(memory_space=pltpu.VMEM)
    return pl.pallas_call(
        kernel,
        out_shape=[jax.ShapeDtypeStruct(a.shape, a.dtype) for a in arrays]
        + [jax.ShapeDtypeStruct((1, heads), F32)],
        in_specs=[local] * count + [local],
        out_specs=[anywhere] * count + [local],
        scratch_shapes=[pltpu.SemaphoreType.DMA((count,))],
    )(*arrays, scales)


def slot_table(anchors, tiles, order, nblocks):
    tiles = tiles.astype(jnp.int32)
    place = order[:, None] * tiles.shape[1] + jnp.arange(tiles.shape[1], dtype=jnp.int32)
    tiles, place = tiles.reshape(-1), place.reshape(-1)
    earlier = (tiles[:, None] == tiles[None, :]) & (place[None, :] < place[:, None])
    before = jnp.max(jnp.where(earlier, place[None, :] + 1, 0), axis=1)
    ids = jnp.arange(nblocks, dtype=jnp.int32)
    last = jnp.max(jnp.where(tiles[None, :] == ids[:, None], place[None, :] + 1, 0), axis=1)
    return jnp.concatenate([tiles, before, last, anchors.astype(jnp.int32)])


def on_device(n, nf, probe, matcher, payload, adjoint, logit_scale, anchor_tiles, sampled_tiles):
    tok, seq_count, total_width = probe.shape
    heads = logit_scale.shape[0]
    width = total_width // heads
    copies = n // (seq_count * heads)
    assert seq_count == 1 and copies * heads == n
    piece = tok // copies
    tile = min(TILE_SPAN, piece)
    units = piece // tile
    n_anchor, n_random = anchor_tiles.shape[1], sampled_tiles.shape[2]
    nblocks = n * tok // TILE_SPAN
    me = lax.axis_index("seq")
    head = me // copies % heads
    unit = jnp.arange(n * units, dtype=jnp.int32)
    order = turn_of(me, unit // units, n) * units + unit % units
    tiles = lax.dynamic_index_in_dim(sampled_tiles, head, 0, False)
    anchors = lax.dynamic_index_in_dim(anchor_tiles, head, 0, False)
    if copies > 1:
        blocks = (unit // units * tok + me % copies * piece + unit % units * tile) // TILE_SPAN
        tiles = jnp.take(tiles, blocks, axis=0)
    table = slot_table(anchors, tiles, order, nblocks)

    dims = (n, nf, copies, tok, piece, tile, width, heads, n_anchor, n_random)
    keys = n * tok
    queries = n * piece
    slots = (3 + n_anchor + n_random) * TILE_SPAN
    chain = (n * units * n_random + 1, TILE_SPAN, width)
    padded = (nblocks + 2, TILE_SPAN, width)
    kept = 2 * (3 * queries + 2 * keys + 2 * nblocks * TILE_SPAN) * width
    kept += 4 * (2 * queries * slots + 2 * math.prod(padded) + 2 * math.prod(chain))
    needed = kept + 10 * 1024 * 1024
    anywhere = pl.BlockSpec(memory_space=pl.ANY)
    scalars = pl.BlockSpec(memory_space=pltpu.SMEM)
    flat = lambda array: array.reshape(tok, total_width)
    tiled = lambda array: array.reshape(tok // TILE_SPAN, TILE_SPAN, total_width)
    parts = jax.ShapeDtypeStruct((tok, n * width), BF16)
    q_out, k_out, v_out, scales = pl.pallas_call(
        functools.partial(attention_kernel, dims),
        out_shape=(
            jax.ShapeDtypeStruct((tok, total_width), BF16),
            parts,
            parts,
            jax.ShapeDtypeStruct((8, 128), F32),
        ),
        in_specs=[pl.BlockSpec(memory_space=pltpu.HBM)] * 4 + [scalars] * 2,
        out_specs=(anywhere, anywhere, anywhere, pl.BlockSpec(memory_space=pltpu.VMEM)),
        scratch_shapes=[
            pltpu.VMEM((queries, width), BF16),
            pltpu.VMEM(padded, BF16),
            pltpu.VMEM(padded, BF16),
            pltpu.VMEM((queries, width), BF16),
            pltpu.VMEM((queries, slots), F32),
            pltpu.VMEM((queries, slots), F32),
            pltpu.VMEM(padded, F32),
            pltpu.VMEM(padded, F32),
            pltpu.VMEM((n_anchor, TILE_SPAN, width), F32),
            pltpu.VMEM((n_anchor, TILE_SPAN, width), F32),
            pltpu.VMEM(chain, F32),
            pltpu.VMEM(chain, F32),
            pltpu.VMEM((queries, width), BF16),
            pltpu.VMEM((keys, width), BF16),
            pltpu.VMEM((keys, width), BF16),
            pltpu.VMEM((8, 128), F32),
            pltpu.VMEM((nf, 8, 128), F32),
            pltpu.VMEM((n, 8, 128), F32),
            pltpu.SemaphoreType.DMA((4,)),
            pltpu.SemaphoreType.DMA((4,)),
            pltpu.SemaphoreType.DMA((3,)),
            pltpu.SemaphoreType.DMA((3,)),
            pltpu.SemaphoreType.DMA((2,)),
            pltpu.SemaphoreType.DMA((2,)),
        ],
        compiler_params=pltpu.CompilerParams(
            collective_id=0, has_side_effects=True, vmem_limit_bytes=needed
        ),
        cost_estimate=pl.CostEstimate(
            flops=10 * queries * slots * width,
            bytes_accessed=14 * tok * total_width,
            transcendentals=queries * slots,
        ),
    )(flat(probe), tiled(matcher), tiled(payload), flat(adjoint), logit_scale, table)

    def combine(received):
        pieces = received.astype(F32).reshape(tok, heads, copies, width)
        return jnp.sum(pieces, axis=2).astype(BF16)

    if copies == 1:
        q_out, k_out, v_out, scales = hand_over((q_out, k_out, v_out), scales, heads)
    else:
        q_out, scales = hand_over((q_out,), scales, heads)
        k_out, v_out = combine(k_out), combine(v_out)
    shaped = lambda array: array.reshape(probe.shape)
    return shaped(q_out), shaped(k_out), shaped(v_out), scales.reshape(heads)


def solution(mesh):
    placed = P("seq", "fsdp", None)
    return jax.shard_map(
        functools.partial(on_device, mesh.shape["seq"], mesh.shape["fsdp"]),
        mesh=mesh,
        in_specs=(placed, placed, placed, placed, P(), P(), P()),
        out_specs=(placed, placed, placed, P()),
        check_vma=False,
    )
```

```python
import functools
import math

import jax
import jax.numpy as jnp
from jax import lax
from jax.experimental import pallas as pl
from jax.experimental.pallas import tpu as pltpu
from jax.sharding import PartitionSpec as P

TILE_SPAN = 64
STRIDE = 5
MASKED = -1e30
MESH = pl.DeviceIdType.MESH
F32 = jnp.float32
BF16 = jnp.bfloat16


def stride_of(n):
    return STRIDE if math.gcd(STRIDE, n) == 1 else 1


def peer_of(me, i, n):
    return (me + i * stride_of(n)) % n


def turn_of(me, peer, n):
    return ((peer - me + n) * pow(stride_of(n), -1, n) + n - 1) % n


def attention_kernel(
    dims,
    q_in,
    k_in,
    v_in,
    g_in,
    scale_in,
    table,
    q_out,
    k_out,
    v_out,
    scale_out,
    qbuf,
    kbuf,
    vbuf,
    gbuf,
    s_ref,
    p_ref,
    dk_acc,
    dv_acc,
    dk_anchor,
    dv_anchor,
    dk_chain,
    dv_chain,
    dq_send,
    dk_send,
    dv_send,
    temp_acc,
    pair_terms,
    item_terms,
    in_send,
    in_recv,
    out_send,
    out_recv,
    term_send,
    term_recv,
):
    n, nf, copies, tok, piece, tile, width, heads, n_anchor, n_random = dims
    span = TILE_SPAN
    nblocks = n * tok // span
    units = piece // tile
    entries = n * units * n_random
    window = 3 * span
    reciprocal = 1.0 / math.sqrt(width)
    me = lax.axis_index("seq")
    mine = lax.axis_index("fsdp")
    item = me // copies
    replica = me % copies
    cols = lambda d: pl.ds(pl.multiple_of(d // copies * width, width), width)

    barrier = pltpu.get_barrier_semaphore()

    def greet(o, _):
        pl.semaphore_signal(
            barrier, inc=1, device_id={"seq": (me + o) % n}, device_id_type=MESH
        )
        return _

    lax.fori_loop(1, n, greet, 0)
    for o in range(1, nf):
        pl.semaphore_signal(
            barrier, inc=1, device_id={"fsdp": (mine + o) % nf}, device_id_type=MESH
        )
    pl.semaphore_wait(barrier, n - 1 + nf - 1)

    arrivals = (
        (k_in, kbuf, tok // span, 1),
        (q_in, qbuf, piece, 0),
        (g_in, gbuf, piece, 0),
        (v_in, vbuf, tok // span, 1),
    )

    def prepare():
        zero_block = jnp.zeros((span, width), BF16)
        for buf in (kbuf, vbuf):
            buf[0] = zero_block
            buf[nblocks + 1] = zero_block

        def clear(c, _):
            dk_acc[c] = jnp.zeros((span, width), F32)
            dv_acc[c] = jnp.zeros((span, width), F32)
            return _

        lax.fori_loop(0, nblocks + 2, clear, 0)
        dk_anchor[...] = jnp.zeros_like(dk_anchor)
        dv_anchor[...] = jnp.zeros_like(dv_anchor)
        dk_chain[0] = jnp.zeros((span, width), F32)
        dv_chain[0] = jnp.zeros((span, width), F32)
        temp_acc[...] = jnp.zeros_like(temp_acc)

    def sent(a):
        _, target, rows, _ = arrivals[a]
        ref = target.at[pl.ds(0, (n - 1) * rows)]
        pltpu.make_async_copy(ref, ref, in_send.at[a]).wait()

    for a, (source, target, rows, shift) in enumerate(arrivals):
        if a == 2:
            prepare()
        if a >= 2:
            sent(a - 2)

        def block(d):
            if shift:
                return source.at[:, :, cols(d)]
            return source.at[pl.ds(pl.multiple_of(d % copies * rows, rows), rows), cols(d)]

        if shift:
            landing = target.at[pl.ds(shift + me * rows, rows)]
        else:
            landing = target.at[pl.ds(pl.multiple_of(me * rows, rows), rows)]

        def send(o, _):
            d = peer_of(me, o, n)
            pltpu.make_async_remote_copy(
                src_ref=block(d),
                dst_ref=landing,
                send_sem=in_send.at[a],
                recv_sem=in_recv.at[a],
                device_id={"seq": d},
                device_id_type=MESH,
            ).start()
            return _

        pltpu.make_async_copy(block(me), landing, in_recv.at[a]).start()
        lax.fori_loop(1, n, send, 0)

    def arrive(a):
        _, target, rows, shift = arrivals[a]
        ref = target.at[pl.ds(shift, n * rows)]
        pltpu.make_async_copy(ref, ref, in_recv.at[a]).wait()

    scale = scale_in[item % heads]
    alpha = scale * reciprocal
    anchors = [table[2 * entries + nblocks + x] for x in range(n_anchor)]
    slots = 3 + n_anchor + n_random
    slot_of = lax.broadcasted_iota(jnp.int32, (1, slots * span), 1) // span

    def unit_at(k, j):
        p = peer_of(me, k + 1, n)
        row = pl.multiple_of(p * piece + j * tile, tile)
        blk = (p * tok + replica * piece + j * tile) // span
        return pl.ds(row, tile), blk, (k * units + j, p * units + j)

    def select(buf, blk, t):
        parts = [buf[pl.ds(blk, 3)].reshape(window, width)]
        for a in anchors:
            parts.append(buf[a + 1])
        for x in range(n_random):
            parts.append(buf[table[t[1] * n_random + x] + 1])
        return jnp.concatenate(parts, axis=0)

    def bias_of(blk):
        off = lambda dead: jnp.where(dead, MASKED, 0.0).astype(F32)
        bias = jnp.where(slot_of == 0, off(blk == 0), 0.0)
        bias = jnp.where(slot_of == 2, off(blk == nblocks - 1), bias)
        for x, a in enumerate(anchors):
            bias = jnp.where(slot_of == 3 + x, off(jnp.abs(a - blk) <= 1), bias)
        return bias

    def scatter(d, blk, t, acc, anchor, chain):
        base = window + n_anchor * span
        acc[pl.ds(blk, 3)] += d[:window].reshape(3, span, width)
        anchor[...] += d[window:base].reshape(n_anchor, span, width)
        for x in range(n_random):
            before = table[entries + t[1] * n_random + x]
            chain[t[0] * n_random + x + 1] = (
                chain[before] + d[base + x * span : base + (x + 1) * span]
            )

    rows_by_cols = (((1,), (1,)), ((), ()))
    over_rows = (((0,), (0,)), ((), ()))

    arrive(0)
    arrive(1)

    group = 2 if units <= 2 else 1
    steps = n // group
    members = lambda i: [(i * group + y, j) for y in range(group) for j in range(units)]

    def scores(i, _):
        for k, j in members(i):
            at, blk, t = unit_at(k, j)
            s = lax.dot_general(
                qbuf[at, :], select(kbuf, blk, t), rows_by_cols, preferred_element_type=F32
            )
            logits = s * alpha + bias_of(blk)
            e = jnp.exp(logits - jnp.max(logits, axis=1, keepdims=True))
            s_ref[at, :] = s
            p_ref[at, :] = e * (1.0 / jnp.sum(e, axis=1, keepdims=True))
        return _

    lax.fori_loop(0, steps, scores, 0)

    arrive(2)

    def value_terms(i, _):
        for k, j in members(i):
            at, blk, t = unit_at(k, j)
            low = p_ref[at, :].astype(BF16)
            dv = lax.dot_general(low, gbuf[at, :], over_rows, preferred_element_type=F32)
            scatter(dv, blk, t, dv_acc, dv_anchor, dv_chain)
        return _

    lax.fori_loop(0, steps, value_terms, 0)

    def send_back(source, rows, target, target_rows, x, k):
        d = peer_of(me, k + 1, n)
        block = source.at[pl.ds(pl.multiple_of(d * rows, rows), rows)]

        @pl.when(k < n - 1)
        def _():
            pltpu.make_async_remote_copy(
                src_ref=block,
                dst_ref=target.at[target_rows, landing_cols[x]],
                send_sem=out_send.at[x],
                recv_sem=out_recv.at[x],
                device_id={"seq": d},
                device_id_type=MESH,
            ).start()

        @pl.when(k == n - 1)
        def _():
            pltpu.make_async_copy(
                source.at[pl.ds(pl.multiple_of(me * rows, rows), rows)],
                target.at[target_rows, landing_cols[x]],
                out_recv.at[x],
            ).start()

    own_part = pl.ds(pl.multiple_of(me * width, width), width)
    landing_cols = (cols(me), own_part, own_part)

    def finish(acc, anchor, chain, source, target, x):
        def step(k, _):
            d = peer_of(me, k + 1, n)
            for b in range(tok // span):
                c = d * (tok // span) + b
                last = table[2 * entries + c]
                total = acc[c + 1] + chain[last]
                for y, a in enumerate(anchors):
                    total += jnp.where(a == c, anchor[y], 0.0)
                source[pl.ds(pl.multiple_of(c * span, span), span), :] = total.astype(BF16)
            send_back(source, tok, target, slice(None), x, k)
            return _

        lax.fori_loop(0, n, step, 0)

    finish(dv_acc, dv_anchor, dv_chain, dv_send, v_out, 2)

    arrive(3)

    def score_terms(i, _):
        for k, j in members(i):
            at, blk, t = unit_at(k, j)
            dprob = lax.dot_general(
                gbuf[at, :], select(vbuf, blk, t), rows_by_cols, preferred_element_type=F32
            )
            prob = p_ref[at, :]
            delta = jnp.sum(prob * dprob, axis=1, keepdims=True)
            dscore = prob * (dprob - delta)
            both = dscore * s_ref[at, :]
            lanes = both[:, :width]
            for y in range(1, slots * span // width):
                lanes += both[:, y * width : (y + 1) * width]
            part = lanes[0:8]
            for y in range(1, tile // 8):
                part += lanes[y * 8 : (y + 1) * 8]
            temp_acc[...] += part
            draw = (dscore * alpha).astype(BF16)
            dq = jnp.dot(draw, select(kbuf, blk, t), preferred_element_type=F32)
            dq_send[at, :] = dq.astype(BF16)
            dk = lax.dot_general(draw, qbuf[at, :], over_rows, preferred_element_type=F32)
            scatter(dk, blk, t, dk_acc, dk_anchor, dk_chain)
        mine_rows = pl.ds(pl.multiple_of(replica * piece, piece), piece)
        for y in range(group):
            send_back(dq_send, piece, q_out, mine_rows, 0, i * group + y)
        return _

    lax.fori_loop(0, steps, score_terms, 0)
    finish(dk_acc, dk_anchor, dk_chain, dk_send, k_out, 1)

    total = jnp.sum(temp_acc[...], axis=1, keepdims=True)
    total = jnp.sum(total, axis=0, keepdims=True) * reciprocal
    pair_terms[mine] = jnp.broadcast_to(total, (8, 128))
    for o in range(1, nf):
        pltpu.make_async_remote_copy(
            src_ref=pair_terms.at[mine],
            dst_ref=pair_terms.at[mine],
            send_sem=term_send.at[0],
            recv_sem=term_recv.at[0],
            device_id={"fsdp": (mine + o) % nf},
            device_id_type=MESH,
        ).start()
    rest = pair_terms.at[pl.ds(0, nf - 1)]
    pltpu.make_async_copy(rest, rest, term_recv.at[0]).wait()
    pltpu.make_async_copy(rest, rest, term_send.at[0]).wait()
    total = pair_terms[0]
    for o in range(1, nf):
        total += pair_terms[o]
    item_terms[me] = total

    def tell(o, _):
        pltpu.make_async_remote_copy(
            src_ref=item_terms.at[me],
            dst_ref=item_terms.at[me],
            send_sem=term_send.at[1],
            recv_sem=term_recv.at[1],
            device_id={"seq": (me + o) % n},
            device_id_type=MESH,
        ).start()
        return _

    lax.fori_loop(1, n, tell, 0)
    rest = item_terms.at[pl.ds(0, n - 1)]
    pltpu.make_async_copy(rest, rest, term_recv.at[1]).wait()
    pltpu.make_async_copy(rest, rest, term_send.at[1]).wait()
    lane = lax.broadcasted_iota(jnp.int32, (8, 128), 1)
    result = jnp.zeros((8, 128), F32)
    for d in range(n):
        result += jnp.where(lane == d // copies % heads, item_terms[d], 0.0)
    scale_out[...] = result

    sent(2)
    sent(3)
    for x, (source, rows, target) in enumerate(
        ((dq_send, piece, q_out), (dk_send, tok, k_out), (dv_send, tok, v_out))
    ):
        ref = source.at[pl.ds(0, (n - 1) * rows)]
        pltpu.make_async_copy(ref, ref, out_send.at[x]).wait()
        pltpu.make_async_copy(target, target, out_recv.at[x]).wait()


def hand_over(arrays, scales, heads):
    count = len(arrays)

    def kernel(*refs):
        sources, scale_ref = refs[:count], refs[count]
        targets, scale_out, sems = refs[count + 1 : -2], refs[-2], refs[-1]
        copies = []
        for x, (source, target) in enumerate(zip(sources, targets)):
            copies.append(pltpu.make_async_copy(source, target, sems.at[x]))
            copies[-1].start()
        scale_out[...] = scale_ref[0:1, :heads]
        for copy in copies:
            copy.wait()

    anywhere = pl.BlockSpec(memory_space=pl.ANY)
    local = pl.BlockSpec(memory_space=pltpu.VMEM)
    return pl.pallas_call(
        kernel,
        out_shape=[jax.ShapeDtypeStruct(a.shape, a.dtype) for a in arrays]
        + [jax.ShapeDtypeStruct((1, heads), F32)],
        in_specs=[local] * count + [local],
        out_specs=[anywhere] * count + [local],
        scratch_shapes=[pltpu.SemaphoreType.DMA((count,))],
    )(*arrays, scales)


def slot_table(anchors, tiles, order, nblocks):
    tiles = tiles.astype(jnp.int32)
    place = order[:, None] * tiles.shape[1] + jnp.arange(tiles.shape[1], dtype=jnp.int32)
    tiles, place = tiles.reshape(-1), place.reshape(-1)
    earlier = (tiles[:, None] == tiles[None, :]) & (place[None, :] < place[:, None])
    before = jnp.max(jnp.where(earlier, place[None, :] + 1, 0), axis=1)
    ids = jnp.arange(nblocks, dtype=jnp.int32)
    last = jnp.max(jnp.where(tiles[None, :] == ids[:, None], place[None, :] + 1, 0), axis=1)
    return jnp.concatenate([tiles, before, last, anchors.astype(jnp.int32)])


def on_device(n, nf, probe, matcher, payload, adjoint, logit_scale, anchor_tiles, sampled_tiles):
    tok, seq_count, total_width = probe.shape
    heads = logit_scale.shape[0]
    width = total_width // heads
    copies = n // (seq_count * heads)
    assert seq_count == 1 and copies * heads == n
    piece = tok // copies
    tile = min(TILE_SPAN, piece)
    units = piece // tile
    n_anchor, n_random = anchor_tiles.shape[1], sampled_tiles.shape[2]
    nblocks = n * tok // TILE_SPAN
    me = lax.axis_index("seq")
    head = me // copies % heads
    unit = jnp.arange(n * units, dtype=jnp.int32)
    order = turn_of(me, unit // units, n) * units + unit % units
    tiles = lax.dynamic_index_in_dim(sampled_tiles, head, 0, False)
    anchors = lax.dynamic_index_in_dim(anchor_tiles, head, 0, False)
    if copies > 1:
        blocks = (unit // units * tok + me % copies * piece + unit % units * tile) // TILE_SPAN
        tiles = jnp.take(tiles, blocks, axis=0)
    table = slot_table(anchors, tiles, order, nblocks)

    dims = (n, nf, copies, tok, piece, tile, width, heads, n_anchor, n_random)
    keys = n * tok
    queries = n * piece
    slots = (3 + n_anchor + n_random) * TILE_SPAN
    chain = (n * units * n_random + 1, TILE_SPAN, width)
    padded = (nblocks + 2, TILE_SPAN, width)
    anywhere = pl.BlockSpec(memory_space=pl.ANY)
    scalars = pl.BlockSpec(memory_space=pltpu.SMEM)
    flat = lambda array: array.reshape(tok, total_width)
    tiled = lambda array: array.reshape(tok // TILE_SPAN, TILE_SPAN, total_width)
    parts = jax.ShapeDtypeStruct((tok, n * width), BF16)
    q_out, k_out, v_out, scales = pl.pallas_call(
        functools.partial(attention_kernel, dims),
        out_shape=(
            jax.ShapeDtypeStruct((tok, total_width), BF16),
            parts,
            parts,
            jax.ShapeDtypeStruct((8, 128), F32),
        ),
        in_specs=[anywhere] * 4 + [scalars] * 2,
        out_specs=(anywhere, anywhere, anywhere, pl.BlockSpec(memory_space=pltpu.VMEM)),
        scratch_shapes=[
            pltpu.VMEM((queries, width), BF16),
            pltpu.VMEM(padded, BF16),
            pltpu.VMEM(padded, BF16),
            pltpu.VMEM((queries, width), BF16),
            pltpu.VMEM((queries, slots), F32),
            pltpu.VMEM((queries, slots), F32),
            pltpu.VMEM(padded, F32),
            pltpu.VMEM(padded, F32),
            pltpu.VMEM((n_anchor, TILE_SPAN, width), F32),
            pltpu.VMEM((n_anchor, TILE_SPAN, width), F32),
            pltpu.VMEM(chain, F32),
            pltpu.VMEM(chain, F32),
            pltpu.VMEM((queries, width), BF16),
            pltpu.VMEM((keys, width), BF16),
            pltpu.VMEM((keys, width), BF16),
            pltpu.VMEM((8, 128), F32),
            pltpu.VMEM((nf, 8, 128), F32),
            pltpu.VMEM((n, 8, 128), F32),
            pltpu.SemaphoreType.DMA((4,)),
            pltpu.SemaphoreType.DMA((4,)),
            pltpu.SemaphoreType.DMA((3,)),
            pltpu.SemaphoreType.DMA((3,)),
            pltpu.SemaphoreType.DMA((2,)),
            pltpu.SemaphoreType.DMA((2,)),
        ],
        compiler_params=pltpu.CompilerParams(
            collective_id=0, has_side_effects=True, vmem_limit_bytes=56 * 1024 * 1024
        ),
        cost_estimate=pl.CostEstimate(
            flops=10 * queries * slots * width,
            bytes_accessed=14 * tok * total_width,
            transcendentals=queries * slots,
        ),
    )(flat(probe), tiled(matcher), tiled(payload), flat(adjoint), logit_scale, table)

    def combine(received):
        pieces = received.astype(F32).reshape(tok, heads, copies, width)
        return jnp.sum(pieces, axis=2).astype(BF16)

    if copies == 1:
        q_out, k_out, v_out, scales = hand_over((q_out, k_out, v_out), scales, heads)
    else:
        q_out, scales = hand_over((q_out,), scales, heads)
        k_out, v_out = combine(k_out), combine(v_out)
    shaped = lambda array: array.reshape(probe.shape)
    return shaped(q_out), shaped(k_out), shaped(v_out), scales.reshape(heads)


def solution(mesh):
    placed = P("seq", "fsdp", None)
    return jax.shard_map(
        functools.partial(on_device, mesh.shape["seq"], mesh.shape["fsdp"]),
        mesh=mesh,
        in_specs=(placed, placed, placed, placed, P(), P(), P()),
        out_specs=(placed, placed, placed, P()),
        check_vma=False,
    )
```
